32 devices in a mesh: dp: 4 (over x, core), ctx: 8 (over z, y).
Axes of the slice: x: 2, y: 2, z: 4, core: 2. Of those that a mesh axis runs over, the one named last changes fastest.
Arguments:
- grad_out: bfloat16 [4096, 4096], P(('dp', 'ctx')), may hold values from -6 to 6
- gate: bfloat16 [4096, 4096], P(('dp', 'ctx')), may hold values from -6 to 6
- conv_in: bfloat16 [4096, 4096], P(('dp', 'ctx')), may hold values from -6 to 6
- filt: bfloat16 [4096, 64], P('dp'), may hold values from -0.75 to 0.75
- doc_end: int32 [4096], P(('dp', 'ctx')), may hold values from 1 to 4096, as said below
Outputs:
- grad_in: bfloat16 [4096, 4096], P(('dp', 'ctx'))
- grad_filt: float32 [4096, 64], P('dp')
The draws below stay inside these ranges and needn't reach their ends.
Inputs may be any that keep to these rules, and one draw needn't show every extreme that they name: doc_end is the same for all rows of one document and larger than the row's own index; no document crosses a multiple of 1024.
All inputs are finite; a program needn't handle non-finite values.
Results may differ from the reference program's by a relative error of at most 0.0049.
Values may be sent and summed in bfloat16 or wider, within the bound.
No kernel may reach another device: no remote copies, remote signals or barrier semaphores. Data moves between devices by JAX's collectives and lax.ppermute only.
A program may use at most 64 MiB of HBM per device.

```python
import jax
import jax.numpy as jnp
from jax import lax

C = 4096
TAPS = 64
TOK_DEV = 128
SEQ = 1024
TOKENS = 4096


def draw_doc_end(key, part):
    positions = jnp.arange(1, TOKENS + 1, dtype=jnp.int32)
    opening = jax.random.randint(key, (TOKENS,), 0, 2 * TOK_DEV) == 0
    opening = opening | (positions % SEQ == 0)
    candidate = jnp.where(opening, positions, TOKENS).astype(jnp.int32)
    return lax.cummin(candidate, axis=0, reverse=True)


def spiked(drawn, rng, source, target, shards_of, factor):
    def block_of(axis_at):
        return (jnp.arange(drawn.shape[axis_at]) // (drawn.shape[axis_at] // shards_of)).reshape((-1,) + (1,) * (drawn.ndim - 1 - axis_at))

    first = jax.random.permutation(rng, shards_of)[block_of(target)]
    far = (block_of(target) + shards_of // 2) % shards_of
    return jnp.where((block_of(source) == first) | (block_of(source) == far), factor * drawn, drawn)


def levels(stream_key, shape, pieces, least, high):
    def one(dim, shards_of):
        draws = jax.random.uniform(jax.random.fold_in(jax.random.fold_in(stream_key, 6), dim), (shards_of,), jnp.float32, least / len(pieces), high / len(pieces))
        return jnp.repeat(jnp.exp(draws), shape[dim] // shards_of).reshape((-1,) + (1,) * (len(shape) - dim - 1))

    level = one(*pieces[0])
    for cut in pieces[1:]:
        level = level * one(*cut)
    return level


def normal_values(rng, extent, scale, most, pieces=(), held_as=jnp.bfloat16):
    loudness = levels(rng, extent, pieces, -0.22, 0.18) if pieces else 1.0
    array = jax.random.normal(rng, extent, jnp.float32) * scale * loudness
    return jnp.minimum(jnp.maximum(array, -most), most).astype(held_as)


def bell_draw_with(key, extent, scale, limit, split, heavy, kind=jnp.bfloat16):
    values = scale * jax.random.normal(key, extent, jnp.float32)
    if split:
        values = values * levels(key, extent, split, -0.22, 0.18)
    return jnp.clip(spiked(values, jax.random.fold_in(key, 3), *heavy), -limit, limit).astype(kind)


def setup_inputs(seed: int = 0) -> dict:
    streams_of = jax.random.split(jax.random.key(seed), 6)
    grad_out = bell_draw_with(streams_of[0], (TOKENS, C), 1.0, 6.0, ((0, 32),), (0, 1, 32, 2.75))
    gate = normal_values(streams_of[1], (TOKENS, C), 1.0, 6.0, ((0, 32),))
    conv_in = normal_values(streams_of[2], (TOKENS, C), 1.0, 6.0, ((0, 32),))
    filt = normal_values(streams_of[3], (C, TAPS), TAPS ** -0.5, 0.75, ((0, 4),))
    doc_end = draw_doc_end(jax.random.fold_in(streams_of[5], 71), 0)
    return {"grad_out": grad_out, "gate": gate, "conv_in": conv_in, "filt": filt, "doc_end": doc_end}


def reference(grad_out, gate, conv_in, filt, doc_end):
    grad_y = (grad_out.astype(jnp.float32) * gate.astype(jnp.float32)).astype(jnp.bfloat16)
    padded = jnp.concatenate([grad_y, jnp.zeros((TAPS, C), jnp.bfloat16)], axis=0)
    filt_cols = filt.astype(jnp.float32).T
    offsets = jnp.arange(TAPS, dtype=jnp.int32)
    local_rows = jnp.arange(TOK_DEV, dtype=jnp.int32)

    def block(carry, which):
        first = (which * TOK_DEV).astype(jnp.int32)
        extended = lax.dynamic_slice_in_dim(padded, first, TOK_DEV + TAPS, 0)
        inputs = lax.dynamic_slice_in_dim(conv_in, first, TOK_DEV, 0).astype(jnp.float32)
        remaining = lax.dynamic_slice_in_dim(doc_end, first, TOK_DEV, 0) - (first + local_rows)
        windows = jax.vmap(lambda offset: lax.dynamic_slice_in_dim(extended, offset, TOK_DEV, 0))(offsets)
        in_document = offsets[:, None] < remaining[None, :]
        windows = jnp.where(in_document[:, :, None], windows.astype(jnp.float32), jnp.float32(0.0))
        grad_block = jnp.sum(windows * filt_cols[:, None, :], axis=0).astype(jnp.bfloat16)
        tap_block = jnp.sum(windows * inputs[None, :, :], axis=1)
        return carry + tap_block, grad_block

    total, grads = lax.scan(block, jnp.zeros((TAPS, C), jnp.float32), jnp.arange(TOKENS // TOK_DEV, dtype=jnp.int32))
    return grads.reshape(TOKENS, C), total.T
```

```python
import math

import jax
import jax.numpy as jnp
from jax import lax
from jax.experimental import pallas as pl
from jax.experimental.pallas import tpu as pltpu
from jax.sharding import PartitionSpec as P

LANE = 128


def half_wave(value):
    square = value * value
    total = jnp.zeros_like(value)
    for power in (13, 11, 9, 7, 5, 3, 1):
        sign = -1.0 if power % 4 == 3 else 1.0
        total = total * square + sign * (2 * math.pi) ** power / math.factorial(power)
    return total * value


def waves(turns):
    size = jnp.abs(turns)
    folded = jnp.minimum(size, 0.5 - size)
    return half_wave(0.25 - size), half_wave(jnp.where(turns < 0.0, -folded, folded))


def two_parts(value):
    high = value.astype(jnp.bfloat16)
    return high, (value - high.astype(jnp.float32)).astype(jnp.bfloat16)


def turns_of(order, offset, size):
    inverse = 1.0 / size.astype(jnp.float32)
    product = (order * offset).astype(jnp.float32)
    whole = jnp.floor(product * inverse + 0.5)
    return (product - whole * size.astype(jnp.float32)) * inverse, inverse


def iota(shape, axis):
    return lax.broadcasted_iota(jnp.int32, shape, axis)


def store_narrow(ref, taps, waves_of):
    bins = ref.shape[0] // 2
    first = iota((bins, 2 * taps), 1) < taps
    for which, wave in enumerate(waves_of):
        high, low = two_parts(wave)
        both = jnp.where(first, high.astype(jnp.float32), low.astype(jnp.float32))
        ref[which * bins:(which + 1) * bins, :] = both.astype(jnp.bfloat16)


def store_back(ref, which, wave):
    count, bins = wave.shape
    ref[0:count, which * bins:(which + 1) * bins], ref[count:2 * count, which * bins:(which + 1) * bins] = two_parts(wave)


def basis_kernel(end_ref, first_ref, rows_ref, taps_ref, input_ref, filter_ref,
                 halo_rows_ref, halo_tail_ref, halo_taps_ref, halo_input_ref, halo_filter_ref, down_ref, across_ref):
    rows, taps = input_ref.shape[0] // 2, filter_ref.shape[0] // 2
    bins = rows
    for ref in (down_ref, across_ref):
        ref[...] = jnp.zeros_like(ref)
        ref[2] = jnp.ones_like(ref[2])

    def document(state):
        start, base, _ = state
        end = jnp.minimum(end_ref[start] - first_ref[0], rows)
        length = end - start
        lags = jnp.minimum(taps, length)
        size = length + lags - 1
        size = size + 1 - lax.rem(size, 2)
        count = (size + 1) // 2
        for ref, axis in ((down_ref, 0), (across_ref, 1)):
            at = iota(ref.shape[1:], axis)
            mine = (at >= base) & (at < base + count)
            for which, value in enumerate((start, end, size, at - base, lags)):
                ref[which] = jnp.where(mine, value, ref[which])
        return end, base + count, start

    start_state = (jnp.int32(0), jnp.int32(0), jnp.int32(0))
    _, _, last_start = lax.while_loop(lambda state: state[0] < rows, document, start_state)

    start, end, size, order, lags = [down_ref[which] for which in range(5)]
    for block in range(rows // LANE):
        at = iota(start.shape, 1) + block * LANE
        inside = (at >= start) & (at < end)
        for which, wave in enumerate(waves(turns_of(order, at - start, size)[0])):
            high, low = two_parts(jnp.where(inside, wave, 0.0))
            below, lanes = which * bins, block * LANE
            rows_ref[below:below + bins, lanes:lanes + LANE] = high
            rows_ref[below:below + bins, rows + lanes:rows + lanes + LANE] = low
    narrow = start[:, 0:2 * taps].shape
    at = iota(narrow, 1)
    at = jnp.where(at < taps, at, at - taps)
    inside = at < lags[:, 0:2 * taps]
    turned = waves(turns_of(order[:, 0:2 * taps], at, size[:, 0:2 * taps])[0])
    store_narrow(taps_ref, taps, [jnp.where(inside, wave, 0.0) for wave in turned])

    start, end, size, order, lags = [across_ref[which, 0:1, :] for which in range(5)]
    for ref, count in ((input_ref, rows), (filter_ref, taps)):
        at = iota((count, bins), 0)
        if ref is input_ref:
            offset, inside = at - start, (at >= start) & (at < end)
        else:
            offset, inside = at, at < lags
        turns, inverse = turns_of(order, offset, size)
        weight = jnp.where(inside, jnp.where(order == 0, inverse, 2.0 * inverse), 0.0)
        for which, wave in enumerate(waves(turns)):
            store_back(ref, which, weight * wave)

    end = jnp.minimum(end_ref[rows - 1] - first_ref[0] - rows, taps - 1)
    begin = jnp.where(end > 0, last_start - (rows - taps), taps)
    size = jnp.full((taps, 2 * taps), 2 * taps - 1, jnp.int32)
    at = iota(size.shape, 1)
    at = jnp.where(at < taps, at, at - taps)
    turned = waves(turns_of(iota(size.shape, 0), at, size)[0])
    store_narrow(halo_taps_ref, taps, turned)
    store_narrow(halo_rows_ref, taps, [jnp.where(at < end, wave, 0.0) for wave in turned])
    store_narrow(halo_tail_ref, taps, [jnp.where(at >= begin, wave, 0.0) for wave in turned])
    size = jnp.full((taps, taps), 2 * taps - 1, jnp.int32)
    at, order = iota(size.shape, 0), iota(size.shape, 1)
    turns, inverse = turns_of(order, at - taps, size)
    weight = jnp.where(at > 0, jnp.where(order == 0, inverse, 2.0 * inverse), 0.0)
    for which, wave in enumerate(waves(turns)):
        store_back(halo_filter_ref, which, weight * wave)
        store_back(halo_input_ref, which, jnp.where(at >= begin, weight * wave, 0.0))


def product(left, right):
    return jnp.dot(left, right, preferred_element_type=jnp.float32)


def transform(basis_ref, twice_ref, value):
    twice(twice_ref, value)
    return product(basis_ref[...], twice_ref[...])


def correlate(left, right, basis_ref, z_ref):
    bins, count = left.shape[0] // 2, basis_ref.shape[0] // 2
    lc, ls, rc, rs = left[:bins], left[bins:], right[:bins], right[bins:]
    z_ref[0, 0:bins, :], z_ref[1, 0:bins, :] = two_parts(lc * rc + ls * rs)
    z_ref[0, bins:, :], z_ref[1, bins:, :] = two_parts(ls * rc - lc * rs)
    both = product(basis_ref[...], z_ref[0])
    return both[:count] + (both[count:] + product(basis_ref[0:count, :], z_ref[1]))


def twice(ref, value):
    count = value.shape[0]
    ref[0:count, :] = value
    ref[count:2 * count, :] = value


def gated(grad_out, gate):
    return (grad_out.astype(jnp.float32) * gate.astype(jnp.float32)).astype(jnp.bfloat16)


def in_turn(count, width, unit):
    together = 2 if count % 2 == 0 else 1

    def step(at, carry):
        for slot in range(together):
            which = at * together + slot
            unit(which, pl.ds(pl.multiple_of(which * width, LANE), width), slot)
        return carry

    lax.fori_loop(0, count // together, step, 0)


def place_pieces(place_ref, pieces, f_ref):
    order = iter(slots(f_ref.shape[0]))
    for piece in pieces:
        for which in range(piece.shape[0]):
            twice(f_ref.at[jnp.bitwise_xor(place_ref[0], next(order))], piece[which])


def own_filter_kernel(rows_ref, filter_ref, grad_out_ref, gate_ref, conv_in_ref, terms_ref, y_ref, x_ref, z_ref):
    width = y_ref.shape[2]

    def unit(which, lanes, slot):
        y_hat = transform(rows_ref, y_ref.at[slot], gated(grad_out_ref[:, lanes], gate_ref[:, lanes]))
        x_hat = transform(rows_ref, x_ref.at[slot], conv_in_ref[:, lanes])
        terms_ref[:, lanes] = correlate(y_hat, x_hat, filter_ref, z_ref.at[slot])

    in_turn(terms_ref.shape[1] // width, width, unit)


def own_input_kernel(place_ref, rows_ref, taps_ref, input_ref, grad_out_ref, gate_ref, *refs):
    pieces, (head_ref, tail_ref, y_ref, f_ref, z_ref) = refs[:-5], refs[-5:]
    channels, width = head_ref.shape[1], y_ref.shape[2]
    place_pieces(place_ref, pieces, f_ref)

    def unit(which, lanes, slot):
        y_hat = transform(rows_ref, y_ref.at[slot], gated(grad_out_ref[:, lanes], gate_ref[:, lanes]))
        grad_in = correlate(y_hat, product(taps_ref[...], f_ref[which]), input_ref, z_ref.at[slot])
        head_ref[:, lanes] = grad_in[:head_ref.shape[0]].astype(head_ref.dtype)
        tail_ref[:, lanes] = grad_in[head_ref.shape[0]:]

    in_turn(channels // width, width, unit)


def halo_filter_kernel(place_ref, rows_ref, tail_ref, filter_ref, own_ref, conv_in_ref, halo_ref, after_ref,
                       keep_ref, send_ref, y_ref, x_ref, z_ref, sum_ref):
    del after_ref
    taps, owners = own_ref.shape[0], y_ref.shape[0]
    rows, width = conv_in_ref.shape[0], y_ref.shape[2]
    for which in range(owners):
        lanes = pl.ds(which * width, width)
        y_hat = transform(rows_ref, y_ref.at[which], halo_ref[:, lanes])
        x_hat = transform(tail_ref, x_ref.at[which], conv_in_ref[rows - taps:, lanes])
        sum_ref[which] = own_ref[:, lanes] + correlate(y_hat, x_hat, filter_ref, z_ref.at[which])
    for pair in range(owners // 2):
        keep_ref[pair] = sum_ref[jnp.bitwise_xor(place_ref[0], 2 * pair)]
        send_ref[pair] = sum_ref[jnp.bitwise_xor(place_ref[0], 2 * pair + 1)].astype(send_ref.dtype)


def halo_input_kernel(place_ref, rows_ref, taps_ref, input_ref, after_ref, halo_ref, head_ref, tail_ref, *refs):
    pieces, (out_ref, passed_ref, y_ref, f_ref, z_ref) = refs[:-5], refs[-5:]
    step = pl.program_id(0)
    head = head_ref.shape[0]

    @pl.when(step == 0)
    def _():
        place_pieces(place_ref, pieces, f_ref)
        passed_ref[...] = after_ref[...]

    y_hat = transform(rows_ref, y_ref, halo_ref[...])
    value = correlate(y_hat, product(taps_ref[...], f_ref[step]), input_ref, z_ref)
    out_ref[0:head, :] = head_ref[...]
    out_ref[head:, :] = (tail_ref[...] + value).astype(out_ref.dtype)


def scalars():
    return pl.BlockSpec(memory_space=pltpu.SMEM)


def whole(array):
    return pl.BlockSpec(array.shape, lambda step: (0,) * len(array.shape))


def tiled(rows, tile, at=0):
    return pl.BlockSpec((rows, tile), lambda step: (at, step))


def scratch(rows, tile):
    return pltpu.VMEM((rows, tile), jnp.bfloat16)


def shaped(*shape, dtype=jnp.bfloat16):
    return jax.ShapeDtypeStruct(shape, dtype)


def params():
    return pltpu.CompilerParams(vmem_limit_bytes=24 * 1024 * 1024)


def cost(flops, moved):
    return pl.CostEstimate(flops=flops, bytes_accessed=moved, transcendentals=0)


def make_basis(doc_end, first, rows, taps):
    own = [shaped(2 * rows, 2 * rows), shaped(2 * rows, 2 * taps), shaped(2 * rows, 2 * rows), shaped(2 * taps, 2 * rows)]
    halo = [shaped(2 * taps, 2 * taps)] * 5
    return pl.pallas_call(
        basis_kernel,
        in_specs=[scalars(), scalars()],
        out_shape=own + halo,
        scratch_shapes=[pltpu.VMEM((5, rows, LANE), jnp.int32), pltpu.VMEM((5, 8, rows), jnp.int32)],
        compiler_params=params(),
        cost_estimate=cost(10000000, 1000000),
        name="basis",
    )(doc_end, first)


def inside(count):
    return [pl.BlockSpec(memory_space=pltpu.VMEM)] * count


def own_filter(bases, grad_out, gate, conv_in, taps, width):
    rows, channels = grad_out.shape
    return pl.pallas_call(
        own_filter_kernel,
        in_specs=inside(5),
        out_specs=inside(1)[0],
        out_shape=shaped(taps, channels, dtype=jnp.float32),
        scratch_shapes=[
            pltpu.VMEM((2, 2 * rows, width), jnp.bfloat16), pltpu.VMEM((2, 2 * rows, width), jnp.bfloat16),
            pltpu.VMEM((2, 2, 2 * rows, width), jnp.bfloat16),
        ],
        compiler_params=params(),
        cost_estimate=cost(20 * rows * rows * channels, (6 * rows + 4 * taps) * channels),
        name="own_filter",
    )(*bases, grad_out, gate, conv_in)


def own_input(place, bases, grad_out, gate, pieces, owners):
    rows, channels = grad_out.shape
    taps, width = pieces[0].shape[1:]
    return pl.pallas_call(
        own_input_kernel,
        in_specs=[scalars(), *inside(5 + len(pieces))],
        out_specs=inside(2),
        out_shape=[shaped(rows - taps, channels), shaped(taps, channels, dtype=jnp.float32)],
        scratch_shapes=[
            pltpu.VMEM((2, 2 * rows, width), jnp.bfloat16), pltpu.VMEM((owners, 2 * taps, width), jnp.bfloat16),
            pltpu.VMEM((2, 2, 2 * rows, width), jnp.bfloat16),
        ],
        compiler_params=params(),
        cost_estimate=cost(30 * rows * rows * channels, (6 * rows + 6 * taps) * channels),
        name="own_input",
    )(place, *bases, grad_out, gate, *pieces)


def halo_filter(place, bases, own, conv_in, halo, after, owners):
    rows, channels = conv_in.shape
    taps = halo.shape[0]
    width = channels // owners
    twice_held = pltpu.VMEM((owners, 2 * taps, width), jnp.bfloat16)
    return pl.pallas_call(
        halo_filter_kernel,
        in_specs=[scalars(), *inside(7)],
        out_specs=inside(2),
        out_shape=[shaped(owners // 2, taps, width, dtype=jnp.float32), shaped(owners // 2, taps, width)],
        scratch_shapes=[
            twice_held, twice_held, pltpu.VMEM((owners, 2, 2 * taps, width), jnp.bfloat16),
            pltpu.VMEM((owners, taps, width), jnp.float32),
        ],
        compiler_params=params(),
        cost_estimate=cost(28 * taps * taps * channels, 10 * taps * channels),
        name="halo_filter",
    )(place, *bases, own, conv_in, halo, after)


def halo_input(place, bases, after, halo, head, tail, pieces, owners):
    taps, channels = halo.shape
    width = channels // owners
    rows = head.shape[0] + taps
    return pl.pallas_call(
        halo_input_kernel,
        grid=(owners,),
        in_specs=[
            scalars(), *[whole(basis) for basis in bases], *inside(1), tiled(taps, width), tiled(rows - taps, width),
            tiled(taps, width), *[whole(piece) for piece in pieces],
        ],
        out_specs=[tiled(rows, width), *inside(1)],
        out_shape=[shaped(rows, channels), shaped(*after.shape, dtype=after.dtype)],
        scratch_shapes=[
            scratch(2 * taps, width), pltpu.VMEM((owners, 2 * taps, width), jnp.bfloat16),
            pltpu.VMEM((2, 2 * taps, width), jnp.bfloat16),
        ],
        compiler_params=params(),
        cost_estimate=cost(28 * taps * taps * channels, 10 * taps * channels),
        name="halo_input",
    )(place, *bases, after, halo, head, tail, *pieces)


def slots(owners):
    order, bit = [0], owners // 2
    while bit:
        order += [m + bit for m in order]
        bit //= 2
    return order


def swap(value, axis, bit):
    return lax.ppermute(value, axis, [(source, source ^ bit) for source in range(lax.axis_size(axis))])


def gather(value, axis):
    held, bit = [value[None]], lax.axis_size(axis) // 2
    while bit:
        held.append(swap(jnp.concatenate(held) if len(held) > 1 else held[0], axis, bit))
        bit //= 2
    return held


def narrow(value):
    return value.astype(jnp.bfloat16)


def widen(value):
    return value.astype(jnp.float32)


def body(grad_out, gate, conv_in, filt, doc_end):
    rows, channels = grad_out.shape
    taps = filt.shape[1]
    dp, ctx = lax.axis_size("dp"), lax.axis_size("ctx")
    owner, block = lax.axis_index("dp"), lax.axis_index("ctx")
    place = owner.reshape(1)
    first_row = ((owner * ctx + block) * rows).reshape(1)

    following = narrow(widen(grad_out[:taps]) * widen(gate[:taps]))
    halo = lax.ppermute(following, "ctx", [(source, source - 1) for source in range(1, ctx)])
    pieces = gather(filt.T, "dp")

    bases = make_basis(doc_end, first_row, rows, taps)
    halo_rows, halo_tail, halo_taps, halo_inverse_input, halo_inverse_filter = bases[4:]
    own = own_filter((bases[0], bases[3]), grad_out, gate, conv_in, taps, channels // dp)
    head, tail = own_input(place, bases[:3], grad_out, gate, pieces, dp)
    keep, send = halo_filter(place, (halo_rows, halo_tail, halo_inverse_filter), own, conv_in, halo, tail, dp)

    arrived, bit = swap(send, "dp", 1), 2
    while bit < dp:
        total = keep + widen(arrived)
        keep, arrived = total[0::2], swap(narrow(total[1::2]), "dp", bit)
        bit *= 2
    grad_in, keep = halo_input(
        place, (halo_rows, halo_taps, halo_inverse_input), keep, halo, head, tail, pieces, dp
    )
    total = (keep + widen(arrived))[0]
    half = taps // 2
    low = lax.rem(block, 2) == 0
    kept = jnp.where(low, total[:half], total[half:])
    total = kept + widen(swap(narrow(jnp.where(low, total[half:], total[:half])), "ctx", 1))
    bit = 2
    while bit < ctx:
        mine = narrow(total)
        total = widen(mine) + widen(swap(mine, "ctx", bit))
        bit *= 2
    mine = narrow(total)
    other = swap(mine, "ctx", 1)
    both = jnp.concatenate([jnp.where(low, mine, other), jnp.where(low, other, mine)])
    return (grad_in, widen(both).T)


def solution(mesh):
    placed = (
        P(("dp", "ctx"), None),
        P(("dp", "ctx"), None),
        P(("dp", "ctx"), None),
        P("dp", None),
        P(("dp", "ctx")),
    )
    return jax.shard_map(
        body,
        mesh=mesh,
        in_specs=placed,
        out_specs=(P(("dp", "ctx"), None), P("dp", None)),
        check_vma=False,
    )
```

```python
import math

import jax
import jax.numpy as jnp
from jax import lax
from jax.experimental import pallas as pl
from jax.experimental.pallas import tpu as pltpu
from jax.sharding import PartitionSpec as P

LANE = 128


def half_wave(value):
    square = value * value
    total = jnp.zeros_like(value)
    for power in (13, 11, 9, 7, 5, 3, 1):
        sign = -1.0 if power % 4 == 3 else 1.0
        total = total * square + sign * (2 * math.pi) ** power / math.factorial(power)
    return total * value


def waves(turns):
    size = jnp.abs(turns)
    folded = jnp.minimum(size, 0.5 - size)
    return half_wave(0.25 - size), half_wave(jnp.where(turns < 0.0, -folded, folded))


def two_parts(value):
    high = value.astype(jnp.bfloat16)
    return high, (value - high.astype(jnp.float32)).astype(jnp.bfloat16)


def turns_of(order, offset, size):
    inverse = 1.0 / size.astype(jnp.float32)
    product = (order * offset).astype(jnp.float32)
    whole = jnp.floor(product * inverse + 0.5)
    return (product - whole * size.astype(jnp.float32)) * inverse, inverse


def iota(shape, axis):
    return lax.broadcasted_iota(jnp.int32, shape, axis)


def store_narrow(ref, taps, waves_of):
    bins = ref.shape[0] // 2
    first = iota((bins, 2 * taps), 1) < taps
    for which, wave in enumerate(waves_of):
        high, low = two_parts(wave)
        both = jnp.where(first, high.astype(jnp.float32), low.astype(jnp.float32))
        ref[which * bins:(which + 1) * bins, :] = both.astype(jnp.bfloat16)


def store_back(ref, which, wave):
    count, bins = wave.shape
    ref[0:count, which * bins:(which + 1) * bins], ref[count:2 * count, which * bins:(which + 1) * bins] = two_parts(wave)


def basis_kernel(end_ref, first_ref, rows_ref, taps_ref, input_ref, filter_ref,
                 halo_rows_ref, halo_tail_ref, halo_taps_ref, halo_input_ref, halo_filter_ref, down_ref, across_ref):
    rows, taps = input_ref.shape[0] // 2, filter_ref.shape[0] // 2
    bins = rows
    for ref in (down_ref, across_ref):
        ref[...] = jnp.zeros_like(ref)
        ref[2] = jnp.ones_like(ref[2])

    def document(state):
        start, base, _ = state
        end = jnp.minimum(end_ref[start] - first_ref[0], rows)
        length = end - start
        lags = jnp.minimum(taps, length)
        size = length + lags - 1
        size = size + 1 - lax.rem(size, 2)
        count = (size + 1) // 2
        for ref, axis in ((down_ref, 0), (across_ref, 1)):
            at = iota(ref.shape[1:], axis)
            mine = (at >= base) & (at < base + count)
            for which, value in enumerate((start, end, size, at - base, lags)):
                ref[which] = jnp.where(mine, value, ref[which])
        return end, base + count, start

    start_state = (jnp.int32(0), jnp.int32(0), jnp.int32(0))
    _, _, last_start = lax.while_loop(lambda state: state[0] < rows, document, start_state)

    start, end, size, order, lags = [down_ref[which] for which in range(5)]
    for block in range(rows // LANE):
        at = iota(start.shape, 1) + block * LANE
        inside = (at >= start) & (at < end)
        for which, wave in enumerate(waves(turns_of(order, at - start, size)[0])):
            high, low = two_parts(jnp.where(inside, wave, 0.0))
            below, lanes = which * bins, block * LANE
            rows_ref[below:below + bins, lanes:lanes + LANE] = high
            rows_ref[below:below + bins, rows + lanes:rows + lanes + LANE] = low
    narrow = start[:, 0:2 * taps].shape
    at = iota(narrow, 1)
    at = jnp.where(at < taps, at, at - taps)
    inside = at < lags[:, 0:2 * taps]
    turned = waves(turns_of(order[:, 0:2 * taps], at, size[:, 0:2 * taps])[0])
    store_narrow(taps_ref, taps, [jnp.where(inside, wave, 0.0) for wave in turned])

    start, end, size, order, lags = [across_ref[which, 0:1, :] for which in range(5)]
    for ref, count in ((input_ref, rows), (filter_ref, taps)):
        at = iota((count, bins), 0)
        if ref is input_ref:
            offset, inside = at - start, (at >= start) & (at < end)
        else:
            offset, inside = at, at < lags
        turns, inverse = turns_of(order, offset, size)
        weight = jnp.where(inside, jnp.where(order == 0, inverse, 2.0 * inverse), 0.0)
        for which, wave in enumerate(waves(turns)):
            store_back(ref, which, weight * wave)

    end = jnp.minimum(end_ref[rows - 1] - first_ref[0] - rows, taps - 1)
    begin = jnp.where(end > 0, last_start - (rows - taps), taps)
    size = jnp.full((taps, 2 * taps), 2 * taps - 1, jnp.int32)
    at = iota(size.shape, 1)
    at = jnp.where(at < taps, at, at - taps)
    turned = waves(turns_of(iota(size.shape, 0), at, size)[0])
    store_narrow(halo_taps_ref, taps, turned)
    store_narrow(halo_rows_ref, taps, [jnp.where(at < end, wave, 0.0) for wave in turned])
    store_narrow(halo_tail_ref, taps, [jnp.where(at >= begin, wave, 0.0) for wave in turned])
    size = jnp.full((taps, taps), 2 * taps - 1, jnp.int32)
    at, order = iota(size.shape, 0), iota(size.shape, 1)
    turns, inverse = turns_of(order, at - taps, size)
    weight = jnp.where(at > 0, jnp.where(order == 0, inverse, 2.0 * inverse), 0.0)
    for which, wave in enumerate(waves(turns)):
        store_back(halo_filter_ref, which, weight * wave)
        store_back(halo_input_ref, which, jnp.where(at >= begin, weight * wave, 0.0))


def product(left, right):
    return jnp.dot(left, right, preferred_element_type=jnp.float32)


def transform(basis_ref, twice_ref, value):
    twice(twice_ref, value)
    return product(basis_ref[...], twice_ref[...])


def correlate(left, right, basis_ref, z_ref):
    bins, count = left.shape[0] // 2, basis_ref.shape[0] // 2
    lc, ls, rc, rs = left[:bins], left[bins:], right[:bins], right[bins:]
    z_ref[0, 0:bins, :], z_ref[1, 0:bins, :] = two_parts(lc * rc + ls * rs)
    z_ref[0, bins:, :], z_ref[1, bins:, :] = two_parts(ls * rc - lc * rs)
    both = product(basis_ref[...], z_ref[0])
    return both[:count] + (both[count:] + product(basis_ref[0:count, :], z_ref[1]))


def twice(ref, value):
    count = value.shape[0]
    ref[0:count, :] = value
    ref[count:2 * count, :] = value


def gated(grad_out, gate):
    return (grad_out.astype(jnp.float32) * gate.astype(jnp.float32)).astype(jnp.bfloat16)


def in_turn(count, width, unit):
    together = 2 if count % 2 == 0 else 1

    def step(at, carry):
        for slot in range(together):
            which = at * together + slot
            unit(which, pl.ds(pl.multiple_of(which * width, LANE), width), slot)
        return carry

    lax.fori_loop(0, count // together, step, 0)


def own_filter_kernel(rows_ref, filter_ref, last_ref, grad_out_ref, gate_ref, conv_in_ref, terms_ref, grad_y_ref, tail_ref,
                      y_ref, x_ref, t_ref, z_ref):
    width, taps, rows = y_ref.shape[2], terms_ref.shape[0], grad_y_ref.shape[0]

    def unit(which, lanes, slot):
        grad_y = gated(grad_out_ref[:, lanes], gate_ref[:, lanes])
        grad_y_ref[:, lanes] = grad_y
        y_hat = transform(rows_ref, y_ref.at[slot], grad_y)
        x_hat = transform(rows_ref, x_ref.at[slot], conv_in_ref[:, lanes])
        tail_ref[:, lanes] = transform(last_ref, t_ref.at[slot], conv_in_ref[rows - taps:, lanes])
        terms_ref[:, lanes] = correlate(y_hat, x_hat, filter_ref, z_ref.at[slot])

    in_turn(terms_ref.shape[1] // width, width, unit)


def own_input_kernel(place_ref, rows_ref, taps_ref, input_ref, grad_y_ref, *refs):
    pieces, (head_ref, tail_ref, filt_ref, y_ref, f_ref, z_ref, sems) = refs[:-7], refs[-7:]
    channels, width = head_ref.shape[1], y_ref.shape[2]
    copies = []
    for m, piece in enumerate(pieces):
        owner = jnp.bitwise_xor(place_ref[0], m)
        lanes = pl.ds(pl.multiple_of(owner * width, LANE), width)
        copies.append(pltpu.make_async_copy(piece, filt_ref.at[:, lanes], sems.at[m]))
        copies[-1].start()
    for copy in copies:
        copy.wait()

    def unit(which, lanes, slot):
        y_hat = transform(rows_ref, y_ref.at[slot], grad_y_ref[:, lanes])
        f_hat = transform(taps_ref, f_ref.at[slot], filt_ref[:, lanes])
        grad_in = correlate(y_hat, f_hat, input_ref, z_ref.at[slot])
        head_ref[:, lanes] = grad_in[:head_ref.shape[0]].astype(head_ref.dtype)
        tail_ref[:, lanes] = grad_in[head_ref.shape[0]:]

    in_turn(channels // width, width, unit)


def halo_filter_kernel(place_ref, rows_ref, filter_ref, own_ref, x_hat_ref, halo_ref, after_ref,
                       keep_ref, send_ref, y_ref, z_ref, sum_ref):
    del after_ref
    owners, _, width = y_ref.shape
    for which in range(owners):
        lanes = pl.ds(which * width, width)
        y_hat = transform(rows_ref, y_ref.at[which], halo_ref[:, lanes])
        sum_ref[which] = own_ref[:, lanes] + correlate(y_hat, x_hat_ref[:, lanes], filter_ref, z_ref.at[which])
    for pair in range(owners // 2):
        keep_ref[pair] = sum_ref[jnp.bitwise_xor(place_ref[0], 2 * pair)]
        send_ref[pair] = sum_ref[jnp.bitwise_xor(place_ref[0], 2 * pair + 1)].astype(send_ref.dtype)


def halo_input_kernel(rows_ref, taps_ref, input_ref, after_ref, halo_ref, head_ref, tail_ref, filt_ref,
                      out_ref, passed_ref, y_ref, f_ref, z_ref, last_ref, sems):
    head, (owners, _, width) = head_ref.shape[0], y_ref.shape
    taps = halo_ref.shape[0]
    copies = [pltpu.make_async_copy(head_ref, out_ref.at[pl.ds(0, head), :], sems.at[owners])]
    copies[0].start()
    passed_ref[...] = after_ref[...]
    for which in range(owners):
        lanes = pl.ds(which * width, width)
        y_hat = transform(rows_ref, y_ref.at[which], halo_ref[:, lanes])
        f_hat = transform(taps_ref, f_ref.at[which], filt_ref[:, lanes])
        value = tail_ref[:, lanes] + correlate(y_hat, f_hat, input_ref, z_ref.at[which])
        last_ref[:, lanes] = value.astype(last_ref.dtype)
        copies.append(pltpu.make_async_copy(
            last_ref.at[:, lanes], out_ref.at[pl.ds(head, taps), lanes], sems.at[which]
        ))
        copies[-1].start()
    for copy in copies:
        copy.wait()


def scalars():
    return pl.BlockSpec(memory_space=pltpu.SMEM)


def shaped(*shape, dtype=jnp.bfloat16):
    return jax.ShapeDtypeStruct(shape, dtype)


def params():
    return pltpu.CompilerParams(vmem_limit_bytes=24 * 1024 * 1024)


def cost(flops, moved):
    return pl.CostEstimate(flops=flops, bytes_accessed=moved, transcendentals=0)


def make_basis(doc_end, first, rows, taps):
    own = [shaped(2 * rows, 2 * rows), shaped(2 * rows, 2 * taps), shaped(2 * rows, 2 * rows), shaped(2 * taps, 2 * rows)]
    halo = [shaped(2 * taps, 2 * taps)] * 5
    return pl.pallas_call(
        basis_kernel,
        in_specs=[scalars(), scalars()],
        out_shape=own + halo,
        scratch_shapes=[pltpu.VMEM((5, rows, LANE), jnp.int32), pltpu.VMEM((5, 8, rows), jnp.int32)],
        compiler_params=params(),
        cost_estimate=cost(10000000, 1000000),
        name="basis",
    )(doc_end, first)


def inside(count):
    return [pl.BlockSpec(memory_space=pltpu.VMEM)] * count


def outside(count):
    return [pl.BlockSpec(memory_space=pltpu.HBM)] * count


def held(*shape):
    return pltpu.VMEM(shape, jnp.bfloat16)


def own_filter(bases, grad_out, gate, conv_in, taps, width):
    rows, channels = grad_out.shape
    return pl.pallas_call(
        own_filter_kernel,
        in_specs=inside(6),
        out_specs=inside(3),
        out_shape=[
            shaped(taps, channels, dtype=jnp.float32), shaped(rows, channels),
            shaped(2 * taps, channels, dtype=jnp.float32),
        ],
        scratch_shapes=[
            held(2, 2 * rows, width), held(2, 2 * rows, width), held(2, 2 * taps, width),
            held(2, 2, 2 * rows, width),
        ],
        compiler_params=params(),
        cost_estimate=cost(20 * rows * rows * channels, (6 * rows + 4 * taps) * channels),
        name="own_filter",
    )(*bases, grad_out, gate, conv_in)


def own_input(place, bases, grad_y, pieces):
    rows, channels = grad_y.shape
    taps, width = pieces[0].shape
    return pl.pallas_call(
        own_input_kernel,
        in_specs=[scalars(), *inside(4), *outside(len(pieces))],
        out_specs=inside(3),
        out_shape=[
            shaped(rows - taps, channels), shaped(taps, channels, dtype=jnp.float32), shaped(taps, channels)
        ],
        scratch_shapes=[
            held(2, 2 * rows, width), held(2, 2 * taps, width), held(2, 2, 2 * rows, width),
            pltpu.SemaphoreType.DMA((len(pieces),)),
        ],
        compiler_params=params(),
        cost_estimate=cost(30 * rows * rows * channels, (6 * rows + 6 * taps) * channels),
        name="own_input",
    )(place, *bases, grad_y, *pieces)


def halo_filter(place, bases, own, x_hat, halo, after, owners):
    taps, channels = halo.shape
    width = channels // owners
    return pl.pallas_call(
        halo_filter_kernel,
        in_specs=[scalars(), *inside(6)],
        out_specs=inside(2),
        out_shape=[shaped(owners // 2, taps, width, dtype=jnp.float32), shaped(owners // 2, taps, width)],
        scratch_shapes=[
            held(owners, 2 * taps, width), held(owners, 2, 2 * taps, width),
            pltpu.VMEM((owners, taps, width), jnp.float32),
        ],
        compiler_params=params(),
        cost_estimate=cost(20 * taps * taps * channels, 10 * taps * channels),
        name="halo_filter",
    )(place, *bases, own, x_hat, halo, after)


def halo_input(bases, after, halo, head, tail, filt, owners):
    taps, channels = halo.shape
    width = channels // owners
    rows = head.shape[0] + taps
    return pl.pallas_call(
        halo_input_kernel,
        in_specs=inside(8),
        out_specs=[pl.BlockSpec(memory_space=pl.ANY), *inside(1)],
        out_shape=[shaped(rows, channels), shaped(*after.shape, dtype=after.dtype)],
        scratch_shapes=[
            held(owners, 2 * taps, width), held(owners, 2 * taps, width), held(owners, 2, 2 * taps, width),
            held(taps, channels), pltpu.SemaphoreType.DMA((owners + 1,)),
        ],
        compiler_params=params(),
        cost_estimate=cost(28 * taps * taps * channels, 10 * taps * channels),
        name="halo_input",
    )(*bases, after, halo, head, tail, filt)


def swap(value, axis, bit):
    return lax.ppermute(value, axis, [(source, source ^ bit) for source in range(lax.axis_size(axis))])


def narrow(value):
    return value.astype(jnp.bfloat16)


def widen(value):
    return value.astype(jnp.float32)


def body(grad_out, gate, conv_in, filt, doc_end):
    rows, channels = grad_out.shape
    taps = filt.shape[1]
    dp, ctx = lax.axis_size("dp"), lax.axis_size("ctx")
    owner, block = lax.axis_index("dp"), lax.axis_index("ctx")
    place = owner.reshape(1)
    first_row = ((owner * ctx + block) * rows).reshape(1)

    following = narrow(widen(grad_out[:taps]) * widen(gate[:taps]))
    halo = lax.ppermute(following, "ctx", [(source, source - 1) for source in range(1, ctx)])
    mine = filt.T
    pieces = [mine] + [swap(mine, "dp", m) for m in range(1, dp)]

    bases = make_basis(doc_end, first_row, rows, taps)
    halo_rows, halo_tail, halo_taps, halo_inverse_input, halo_inverse_filter = bases[4:]
    own, grad_y, x_hat = own_filter((bases[0], bases[3], halo_tail), grad_out, gate, conv_in, taps, channels // dp)
    head, tail, whole_filter = own_input(place, bases[:3], grad_y, pieces)
    keep, send = halo_filter(place, (halo_rows, halo_inverse_filter), own, x_hat, halo, tail, dp)

    arrived, bit = swap(send, "dp", 1), 2
    while bit < dp:
        total = keep + widen(arrived)
        keep, arrived = total[0::2], swap(narrow(total[1::2]), "dp", bit)
        bit *= 2
    grad_in, keep = halo_input(
        (halo_rows, halo_taps, halo_inverse_input), keep, halo, head, tail, whole_filter, dp
    )
    total = (keep + widen(arrived))[0]
    half = taps // 2
    low = lax.rem(block, 2) == 0
    kept = jnp.where(low, total[:half], total[half:])
    total = kept + widen(swap(narrow(jnp.where(low, total[half:], total[:half])), "ctx", 1))
    bit = 2
    while bit < ctx:
        mine = narrow(total)
        total = widen(mine) + widen(swap(mine, "ctx", bit))
        bit *= 2
    mine = narrow(total)
    other = swap(mine, "ctx", 1)
    both = jnp.concatenate([jnp.where(low, mine, other), jnp.where(low, other, mine)])
    return (grad_in, widen(both).T)


def solution(mesh):
    placed = (
        P(("dp", "ctx"), None),
        P(("dp", "ctx"), None),
        P(("dp", "ctx"), None),
        P("dp", None),
        P(("dp", "ctx")),
    )
    return jax.shard_map(
        body,
        mesh=mesh,
        in_specs=placed,
        out_specs=(P(("dp", "ctx"), None), P("dp", None)),
        check_vma=False,
    )
```

```python
import math

import jax
import jax.numpy as jnp
from jax import lax
from jax.experimental import pallas as pl
from jax.experimental.pallas import tpu as pltpu
from jax.sharding import PartitionSpec as P

LANE = 128


def half_wave(value):
    square = value * value
    total = jnp.zeros_like(value)
    for power in (13, 11, 9, 7, 5, 3, 1):
        sign = -1.0 if power % 4 == 3 else 1.0
        total = total * square + sign * (2 * math.pi) ** power / math.factorial(power)
    return total * value


def waves(turns):
    size = jnp.abs(turns)
    folded = jnp.minimum(size, 0.5 - size)
    return half_wave(0.25 - size), half_wave(jnp.where(turns < 0.0, -folded, folded))


def two_parts(value):
    high = value.astype(jnp.bfloat16)
    return high, (value - high.astype(jnp.float32)).astype(jnp.bfloat16)


def turns_of(order, offset, size):
    inverse = 1.0 / size.astype(jnp.float32)
    product = (order * offset).astype(jnp.float32)
    whole = jnp.floor(product * inverse + 0.5)
    return (product - whole * size.astype(jnp.float32)) * inverse, inverse


def iota(shape, axis):
    return lax.broadcasted_iota(jnp.int32, shape, axis)


def store_narrow(ref, taps, waves_of):
    bins = ref.shape[0] // 2
    first = iota((bins, 2 * taps), 1) < taps
    for which, wave in enumerate(waves_of):
        high, low = two_parts(wave)
        both = jnp.where(first, high.astype(jnp.float32), low.astype(jnp.float32))
        ref[which * bins:(which + 1) * bins, :] = both.astype(jnp.bfloat16)


def store_back(ref, which, wave):
    count, bins = wave.shape
    ref[0:count, which * bins:(which + 1) * bins], ref[count:2 * count, which * bins:(which + 1) * bins] = two_parts(wave)


def basis_kernel(end_ref, first_ref, rows_ref, taps_ref, input_ref, filter_ref,
                 halo_rows_ref, halo_tail_ref, halo_taps_ref, halo_input_ref, halo_filter_ref, down_ref, across_ref):
    rows, taps = input_ref.shape[0] // 2, filter_ref.shape[0] // 2
    bins = rows
    for ref in (down_ref, across_ref):
        ref[...] = jnp.zeros_like(ref)
        ref[2] = jnp.ones_like(ref[2])

    def document(state):
        start, base, _ = state
        end = jnp.minimum(end_ref[start] - first_ref[0], rows)
        length = end - start
        lags = jnp.minimum(taps, length)
        size = length + lags - 1
        size = size + 1 - lax.rem(size, 2)
        count = (size + 1) // 2
        for ref, axis in ((down_ref, 0), (across_ref, 1)):
            at = iota(ref.shape[1:], axis)
            mine = (at >= base) & (at < base + count)
            for which, value in enumerate((start, end, size, at - base, lags)):
                ref[which] = jnp.where(mine, value, ref[which])
        return end, base + count, start

    start_state = (jnp.int32(0), jnp.int32(0), jnp.int32(0))
    _, _, last_start = lax.while_loop(lambda state: state[0] < rows, document, start_state)

    start, end, size, order, lags = [down_ref[which] for which in range(5)]
    for block in range(rows // LANE):
        at = iota(start.shape, 1) + block * LANE
        inside = (at >= start) & (at < end)
        for which, wave in enumerate(waves(turns_of(order, at - start, size)[0])):
            high, low = two_parts(jnp.where(inside, wave, 0.0))
            below, lanes = which * bins, block * LANE
            rows_ref[below:below + bins, lanes:lanes + LANE] = high
            rows_ref[below:below + bins, rows + lanes:rows + lanes + LANE] = low
    narrow = start[:, 0:2 * taps].shape
    at = iota(narrow, 1)
    at = jnp.where(at < taps, at, at - taps)
    inside = at < lags[:, 0:2 * taps]
    turned = waves(turns_of(order[:, 0:2 * taps], at, size[:, 0:2 * taps])[0])
    store_narrow(taps_ref, taps, [jnp.where(inside, wave, 0.0) for wave in turned])

    start, end, size, order, lags = [across_ref[which, 0:1, :] for which in range(5)]
    for ref, count in ((input_ref, rows), (filter_ref, taps)):
        at = iota((count, bins), 0)
        if ref is input_ref:
            offset, inside = at - start, (at >= start) & (at < end)
        else:
            offset, inside = at, at < lags
        turns, inverse = turns_of(order, offset, size)
        weight = jnp.where(inside, jnp.where(order == 0, inverse, 2.0 * inverse), 0.0)
        for which, wave in enumerate(waves(turns)):
            store_back(ref, which, weight * wave)

    end = jnp.minimum(end_ref[rows - 1] - first_ref[0] - rows, taps - 1)
    begin = jnp.where(end > 0, last_start - (rows - taps), taps)
    size = jnp.full((taps, 2 * taps), 2 * taps - 1, jnp.int32)
    at = iota(size.shape, 1)
    at = jnp.where(at < taps, at, at - taps)
    turned = waves(turns_of(iota(size.shape, 0), at, size)[0])
    store_narrow(halo_taps_ref, taps, turned)
    store_narrow(halo_rows_ref, taps, [jnp.where(at < end, wave, 0.0) for wave in turned])
    store_narrow(halo_tail_ref, taps, [jnp.where(at >= begin, wave, 0.0) for wave in turned])
    size = jnp.full((taps, taps), 2 * taps - 1, jnp.int32)
    at, order = iota(size.shape, 0), iota(size.shape, 1)
    turns, inverse = turns_of(order, at - taps, size)
    weight = jnp.where(at > 0, jnp.where(order == 0, inverse, 2.0 * inverse), 0.0)
    for which, wave in enumerate(waves(turns)):
        store_back(halo_filter_ref, which, weight * wave)
        store_back(halo_input_ref, which, jnp.where(at >= begin, weight * wave, 0.0))


def product(left, right):
    return jnp.dot(left, right, preferred_element_type=jnp.float32)


def transform(basis_ref, twice_ref, value):
    twice(twice_ref, value)
    return product(basis_ref[...], twice_ref[...])


def correlate(left, right, basis_ref, z_ref):
    bins, count = left.shape[0] // 2, basis_ref.shape[0] // 2
    lc, ls, rc, rs = left[:bins], left[bins:], right[:bins], right[bins:]
    z_ref[0, 0:bins, :], z_ref[1, 0:bins, :] = two_parts(lc * rc + ls * rs)
    z_ref[0, bins:, :], z_ref[1, bins:, :] = two_parts(ls * rc - lc * rs)
    both = product(basis_ref[...], z_ref[0])
    return both[:count] + (both[count:] + product(basis_ref[0:count, :], z_ref[1]))


def twice(ref, value):
    count = value.shape[0]
    ref[0:count, :] = value
    ref[count:2 * count, :] = value


def gated(grad_out, gate):
    return (grad_out.astype(jnp.float32) * gate.astype(jnp.float32)).astype(jnp.bfloat16)


def in_turn(count, width, unit):
    together = 2 if count % 2 == 0 else 1

    def step(at, carry):
        for slot in range(together):
            which = at * together + slot
            unit(which, pl.ds(pl.multiple_of(which * width, LANE), width), slot)
        return carry

    lax.fori_loop(0, count // together, step, 0)


def own_filter_kernel(rows_ref, filter_ref, last_ref, grad_out_ref, gate_ref, conv_in_ref, terms_ref, grad_y_ref, tail_ref,
                      y_ref, x_ref, t_ref, z_ref):
    width, taps, rows = y_ref.shape[2], terms_ref.shape[0], grad_y_ref.shape[0]

    def unit(which, lanes, slot):
        grad_y = gated(grad_out_ref[:, lanes], gate_ref[:, lanes])
        grad_y_ref[:, lanes] = grad_y
        y_hat = transform(rows_ref, y_ref.at[slot], grad_y)
        x_hat = transform(rows_ref, x_ref.at[slot], conv_in_ref[:, lanes])
        tail_ref[:, lanes] = transform(last_ref, t_ref.at[slot], conv_in_ref[rows - taps:, lanes])
        terms_ref[:, lanes] = correlate(y_hat, x_hat, filter_ref, z_ref.at[slot])

    in_turn(terms_ref.shape[1] // width, width, unit)


def own_input_kernel(place_ref, rows_ref, taps_ref, input_ref, grad_y_ref, *refs):
    pieces, (head_ref, tail_ref, filt_ref, y_ref, f_ref, z_ref, sems) = refs[:-7], refs[-7:]
    channels, width = head_ref.shape[1], y_ref.shape[2]
    copies = []
    for m, piece in enumerate(pieces):
        owner = jnp.bitwise_xor(place_ref[0], m)
        lanes = pl.ds(pl.multiple_of(owner * width, LANE), width)
        copies.append(pltpu.make_async_copy(piece, filt_ref.at[:, lanes], sems.at[m]))
        copies[-1].start()
    for copy in copies:
        copy.wait()

    def unit(which, lanes, slot):
        y_hat = transform(rows_ref, y_ref.at[slot], grad_y_ref[:, lanes])
        f_hat = transform(taps_ref, f_ref.at[slot], filt_ref[:, lanes])
        grad_in = correlate(y_hat, f_hat, input_ref, z_ref.at[slot])
        head_ref[:, lanes] = grad_in[:head_ref.shape[0]].astype(head_ref.dtype)
        tail_ref[:, lanes] = grad_in[head_ref.shape[0]:]

    in_turn(channels // width, width, unit)


def halo_filter_kernel(place_ref, rows_ref, filter_ref, own_ref, x_hat_ref, halo_ref, after_ref,
                       keep_ref, send_ref, y_ref, z_ref, sum_ref):
    del after_ref
    owners, _, width = y_ref.shape
    for which in range(owners):
        lanes = pl.ds(which * width, width)
        y_hat = transform(rows_ref, y_ref.at[which], halo_ref[:, lanes])
        sum_ref[which] = own_ref[:, lanes] + correlate(y_hat, x_hat_ref[:, lanes], filter_ref, z_ref.at[which])
    for pair in range(owners // 2):
        keep_ref[pair] = sum_ref[jnp.bitwise_xor(place_ref[0], 2 * pair)]
        send_ref[pair] = sum_ref[jnp.bitwise_xor(place_ref[0], 2 * pair + 1)].astype(send_ref.dtype)


def halo_input_kernel(rows_ref, taps_ref, input_ref, after_ref, halo_ref, head_ref, tail_ref, filt_ref,
                      out_ref, passed_ref, y_ref, f_ref, z_ref, last_ref, sems):
    head, (owners, _, width) = head_ref.shape[0], y_ref.shape
    taps = halo_ref.shape[0]
    copies = [pltpu.make_async_copy(head_ref, out_ref.at[pl.ds(0, head), :], sems.at[owners])]
    copies[0].start()
    passed_ref[...] = after_ref[...]
    for which in range(owners):
        lanes = pl.ds(which * width, width)
        y_hat = transform(rows_ref, y_ref.at[which], halo_ref[:, lanes])
        f_hat = transform(taps_ref, f_ref.at[which], filt_ref[:, lanes])
        value = tail_ref[:, lanes] + correlate(y_hat, f_hat, input_ref, z_ref.at[which])
        last_ref[:, lanes] = value.astype(last_ref.dtype)
        copies.append(pltpu.make_async_copy(
            last_ref.at[:, lanes], out_ref.at[pl.ds(head, taps), lanes], sems.at[which]
        ))
        copies[-1].start()
    for copy in copies:
        copy.wait()


def scalars():
    return pl.BlockSpec(memory_space=pltpu.SMEM)


def shaped(*shape, dtype=jnp.bfloat16):
    return jax.ShapeDtypeStruct(shape, dtype)


def params():
    return pltpu.CompilerParams(vmem_limit_bytes=14 * 1024 * 1024)


def cost(flops, moved):
    return pl.CostEstimate(flops=flops, bytes_accessed=moved, transcendentals=0)


def make_basis(doc_end, first, rows, taps):
    own = [shaped(2 * rows, 2 * rows), shaped(2 * rows, 2 * taps), shaped(2 * rows, 2 * rows), shaped(2 * taps, 2 * rows)]
    halo = [shaped(2 * taps, 2 * taps)] * 5
    return pl.pallas_call(
        basis_kernel,
        in_specs=[scalars(), scalars()],
        out_shape=own + halo,
        scratch_shapes=[pltpu.VMEM((5, rows, LANE), jnp.int32), pltpu.VMEM((5, 8, rows), jnp.int32)],
        compiler_params=params(),
        cost_estimate=cost(1500000000, 1000000),
        name="basis",
    )(doc_end, first)


def inside(count):
    return [pl.BlockSpec(memory_space=pltpu.VMEM)] * count


def outside(count):
    return [pl.BlockSpec(memory_space=pltpu.HBM)] * count


def held(*shape):
    return pltpu.VMEM(shape, jnp.bfloat16)


def own_filter(bases, grad_out, gate, conv_in, taps, width):
    rows, channels = grad_out.shape
    return pl.pallas_call(
        own_filter_kernel,
        in_specs=inside(6),
        out_specs=inside(3),
        out_shape=[
            shaped(taps, channels, dtype=jnp.float32), shaped(rows, channels),
            shaped(2 * taps, channels, dtype=jnp.float32),
        ],
        scratch_shapes=[
            held(2, 2 * rows, width), held(2, 2 * rows, width), held(2, 2 * taps, width),
            held(2, 2, 2 * rows, width),
        ],
        compiler_params=params(),
        cost_estimate=cost(20 * rows * rows * channels, (6 * rows + 4 * taps) * channels),
        name="own_filter",
    )(*bases, grad_out, gate, conv_in)


def own_input(place, bases, grad_y, pieces):
    rows, channels = grad_y.shape
    taps, width = pieces[0].shape
    return pl.pallas_call(
        own_input_kernel,
        in_specs=[scalars(), *inside(4), *outside(len(pieces))],
        out_specs=inside(3),
        out_shape=[
            shaped(rows - taps, channels), shaped(taps, channels, dtype=jnp.float32), shaped(taps, channels)
        ],
        scratch_shapes=[
            held(2, 2 * rows, width), held(2, 2 * taps, width), held(2, 2, 2 * rows, width),
            pltpu.SemaphoreType.DMA((len(pieces),)),
        ],
        compiler_params=params(),
        cost_estimate=cost(30 * rows * rows * channels, (6 * rows + 6 * taps) * channels),
        name="own_input",
    )(place, *bases, grad_y, *pieces)


def halo_filter(place, bases, own, x_hat, halo, after, owners):
    taps, channels = halo.shape
    width = channels // owners
    return pl.pallas_call(
        halo_filter_kernel,
        in_specs=[scalars(), *inside(6)],
        out_specs=inside(2),
        out_shape=[shaped(owners // 2, taps, width, dtype=jnp.float32), shaped(owners // 2, taps, width)],
        scratch_shapes=[
            held(owners, 2 * taps, width), held(owners, 2, 2 * taps, width),
            pltpu.VMEM((owners, taps, width), jnp.float32),
        ],
        compiler_params=params(),
        cost_estimate=cost(20 * taps * taps * channels, 10 * taps * channels),
        name="halo_filter",
    )(place, *bases, own, x_hat, halo, after)


def halo_input(bases, after, halo, head, tail, filt, owners):
    taps, channels = halo.shape
    width = channels // owners
    rows = head.shape[0] + taps
    return pl.pallas_call(
        halo_input_kernel,
        in_specs=inside(8),
        out_specs=[pl.BlockSpec(memory_space=pl.ANY), *inside(1)],
        out_shape=[shaped(rows, channels), shaped(*after.shape, dtype=after.dtype)],
        scratch_shapes=[
            held(owners, 2 * taps, width), held(owners, 2 * taps, width), held(owners, 2, 2 * taps, width),
            held(taps, channels), pltpu.SemaphoreType.DMA((owners + 1,)),
        ],
        compiler_params=params(),
        cost_estimate=cost(28 * taps * taps * channels, 10 * taps * channels),
        name="halo_input",
    )(*bases, after, halo, head, tail, filt)


def swap(value, axis, bit):
    return lax.ppermute(value, axis, [(source, source ^ bit) for source in range(lax.axis_size(axis))])


def narrow(value):
    return value.astype(jnp.bfloat16)


def widen(value):
    return value.astype(jnp.float32)


def body(grad_out, gate, conv_in, filt, doc_end):
    rows, channels = grad_out.shape
    taps = filt.shape[1]
    dp, ctx = lax.axis_size("dp"), lax.axis_size("ctx")
    owner, block = lax.axis_index("dp"), lax.axis_index("ctx")
    place = owner.reshape(1)
    first_row = ((owner * ctx + block) * rows).reshape(1)

    following = narrow(widen(grad_out[:taps]) * widen(gate[:taps]))
    halo = lax.ppermute(following, "ctx", [(source, source - 1) for source in range(1, ctx)])
    mine = filt.T
    pieces = [mine] + [swap(mine, "dp", m) for m in range(1, dp)]

    bases = make_basis(doc_end, first_row, rows, taps)
    halo_rows, halo_tail, halo_taps, halo_inverse_input, halo_inverse_filter = bases[4:]
    own, grad_y, x_hat = own_filter((bases[0], bases[3], halo_tail), grad_out, gate, conv_in, taps, channels // dp)
    head, tail, whole_filter = own_input(place, bases[:3], grad_y, pieces)
    keep, send = halo_filter(place, (halo_rows, halo_inverse_filter), own, x_hat, halo, tail, dp)

    arrived, bit = swap(send, "dp", 1), 2
    while bit < dp:
        total = keep + widen(arrived)
        keep, arrived = total[0::2], swap(narrow(total[1::2]), "dp", bit)
        bit *= 2
    grad_in, keep = halo_input(
        (halo_rows, halo_taps, halo_inverse_input), keep, halo, head, tail, whole_filter, dp
    )
    total = (keep + widen(arrived))[0]
    half = taps // 2
    low = lax.rem(block, 2) == 0
    kept = jnp.where(low, total[:half], total[half:])
    total = kept + widen(swap(narrow(jnp.where(low, total[half:], total[:half])), "ctx", 1))
    bit = 2
    while bit < ctx:
        mine = narrow(total)
        total = widen(mine) + widen(swap(mine, "ctx", bit))
        bit *= 2
    mine = narrow(total)
    other = swap(mine, "ctx", 1)
    both = jnp.concatenate([jnp.where(low, mine, other), jnp.where(low, other, mine)])
    return (grad_in, widen(both).T)


def solution(mesh):
    placed = (
        P(("dp", "ctx"), None),
        P(("dp", "ctx"), None),
        P(("dp", "ctx"), None),
        P("dp", None),
        P(("dp", "ctx")),
    )
    return jax.shard_map(
        body,
        mesh=mesh,
        in_specs=placed,
        out_specs=(P(("dp", "ctx"), None), P("dp", None)),
        check_vma=False,
    )
```

```python
import math

import jax
import jax.numpy as jnp
from jax import lax
from jax.experimental import pallas as pl
from jax.experimental.pallas import tpu as pltpu
from jax.sharding import PartitionSpec as P

LANE = 128


def half_wave(value):
    square = value * value
    total = jnp.zeros_like(value)
    for power in (13, 11, 9, 7, 5, 3, 1):
        sign = -1.0 if power % 4 == 3 else 1.0
        total = total * square + sign * (2 * math.pi) ** power / math.factorial(power)
    return total * value


def waves(turns):
    size = jnp.abs(turns)
    folded = jnp.minimum(size, 0.5 - size)
    return half_wave(0.25 - size), half_wave(jnp.where(turns < 0.0, -folded, folded))


def two_parts(value):
    high = value.astype(jnp.bfloat16)
    return high, (value - high.astype(jnp.float32)).astype(jnp.bfloat16)


def turns_of(order, offset, size):
    inverse = 1.0 / size.astype(jnp.float32)
    product = (order * offset).astype(jnp.float32)
    whole = jnp.floor(product * inverse + 0.5)
    return (product - whole * size.astype(jnp.float32)) * inverse, inverse


def iota(shape, axis):
    return lax.broadcasted_iota(jnp.int32, shape, axis)


def store_narrow(ref, taps, waves_of):
    bins = ref.shape[0] // 2
    first = iota((bins, 2 * taps), 1) < taps
    for which, wave in enumerate(waves_of):
        high, low = two_parts(wave)
        both = jnp.where(first, high.astype(jnp.float32), low.astype(jnp.float32))
        ref[which * bins:(which + 1) * bins, :] = both.astype(jnp.bfloat16)


def store_back(ref, which, wave):
    count, bins = wave.shape
    ref[0:count, which * bins:(which + 1) * bins], ref[count:2 * count, which * bins:(which + 1) * bins] = two_parts(wave)


def basis_kernel(end_ref, first_ref, rows_ref, taps_ref, input_ref, filter_ref,
                 halo_rows_ref, halo_tail_ref, halo_taps_ref, halo_input_ref, halo_filter_ref, down_ref, across_ref):
    rows, taps = input_ref.shape[0] // 2, filter_ref.shape[0] // 2
    bins = rows
    for ref in (down_ref, across_ref):
        ref[...] = jnp.zeros_like(ref)
        ref[2] = jnp.ones_like(ref[2])

    def document(state):
        start, base, _ = state
        end = jnp.minimum(end_ref[start] - first_ref[0], rows)
        length = end - start
        lags = jnp.minimum(taps, length)
        size = length + lags - 1
        size = size + 1 - lax.rem(size, 2)
        count = (size + 1) // 2
        for ref, axis in ((down_ref, 0), (across_ref, 1)):
            at = iota(ref.shape[1:], axis)
            mine = (at >= base) & (at < base + count)
            for which, value in enumerate((start, end, size, at - base, lags)):
                ref[which] = jnp.where(mine, value, ref[which])
        return end, base + count, start

    start_state = (jnp.int32(0), jnp.int32(0), jnp.int32(0))
    _, _, last_start = lax.while_loop(lambda state: state[0] < rows, document, start_state)

    start, end, size, order, lags = [down_ref[which] for which in range(5)]
    for block in range(rows // LANE):
        at = iota(start.shape, 1) + block * LANE
        inside = (at >= start) & (at < end)
        for which, wave in enumerate(waves(turns_of(order, at - start, size)[0])):
            high, low = two_parts(jnp.where(inside, wave, 0.0))
            below, lanes = which * bins, block * LANE
            rows_ref[below:below + bins, lanes:lanes + LANE] = high
            rows_ref[below:below + bins, rows + lanes:rows + lanes + LANE] = low
    narrow = start[:, 0:2 * taps].shape
    at = iota(narrow, 1)
    at = jnp.where(at < taps, at, at - taps)
    inside = at < lags[:, 0:2 * taps]
    turned = waves(turns_of(order[:, 0:2 * taps], at, size[:, 0:2 * taps])[0])
    store_narrow(taps_ref, taps, [jnp.where(inside, wave, 0.0) for wave in turned])

    start, end, size, order, lags = [across_ref[which, 0:1, :] for which in range(5)]
    for ref, count in ((input_ref, rows), (filter_ref, taps)):
        at = iota((count, bins), 0)
        if ref is input_ref:
            offset, inside = at - start, (at >= start) & (at < end)
        else:
            offset, inside = at, at < lags
        turns, inverse = turns_of(order, offset, size)
        weight = jnp.where(inside, jnp.where(order == 0, inverse, 2.0 * inverse), 0.0)
        for which, wave in enumerate(waves(turns)):
            store_back(ref, which, weight * wave)

    end = jnp.minimum(end_ref[rows - 1] - first_ref[0] - rows, taps - 1)
    begin = jnp.where(end > 0, last_start - (rows - taps), taps)
    size = jnp.full((taps, 2 * taps), 2 * taps - 1, jnp.int32)
    at = iota(size.shape, 1)
    at = jnp.where(at < taps, at, at - taps)
    turned = waves(turns_of(iota(size.shape, 0), at, size)[0])
    store_narrow(halo_taps_ref, taps, turned)
    store_narrow(halo_rows_ref, taps, [jnp.where(at < end, wave, 0.0) for wave in turned])
    store_narrow(halo_tail_ref, taps, [jnp.where(at >= begin, wave, 0.0) for wave in turned])
    size = jnp.full((taps, taps), 2 * taps - 1, jnp.int32)
    at, order = iota(size.shape, 0), iota(size.shape, 1)
    turns, inverse = turns_of(order, at - taps, size)
    weight = jnp.where(at > 0, jnp.where(order == 0, inverse, 2.0 * inverse), 0.0)
    for which, wave in enumerate(waves(turns)):
        store_back(halo_filter_ref, which, weight * wave)
        store_back(halo_input_ref, which, jnp.where(at >= begin, weight * wave, 0.0))


def product(left, right):
    return jnp.dot(left, right, preferred_element_type=jnp.float32)


def transform(basis_ref, twice_ref, value):
    twice(twice_ref, value)
    return product(basis_ref[...], twice_ref[...])


def correlate(left, right, basis_ref, z_ref):
    bins, count = left.shape[0] // 2, basis_ref.shape[0] // 2
    lc, ls, rc, rs = left[:bins], left[bins:], right[:bins], right[bins:]
    z_ref[0, 0:bins, :], z_ref[1, 0:bins, :] = two_parts(lc * rc + ls * rs)
    z_ref[0, bins:, :], z_ref[1, bins:, :] = two_parts(ls * rc - lc * rs)
    both = product(basis_ref[...], z_ref[0])
    return both[:count] + (both[count:] + product(basis_ref[0:count, :], z_ref[1]))


def twice(ref, value):
    count = value.shape[0]
    ref[0:count, :] = value
    ref[count:2 * count, :] = value


def gated(grad_out, gate):
    return (grad_out.astype(jnp.float32) * gate.astype(jnp.float32)).astype(jnp.bfloat16)


def in_turn(count, width, unit):
    together = 2 if count % 2 == 0 else 1

    def step(at, carry):
        for slot in range(together):
            which = at * together + slot
            unit(which, pl.ds(pl.multiple_of(which * width, LANE), width), slot)
        return carry

    lax.fori_loop(0, count // together, step, 0)


def own_filter_kernel(rows_ref, filter_ref, last_ref, grad_out_ref, gate_ref, conv_in_ref, terms_ref, grad_y_ref, tail_ref,
                      y_ref, x_ref, t_ref, z_ref):
    width, taps, rows = y_ref.shape[2], terms_ref.shape[0], grad_y_ref.shape[0]

    def unit(which, lanes, slot):
        grad_y = gated(grad_out_ref[:, lanes], gate_ref[:, lanes])
        grad_y_ref[:, lanes] = grad_y
        y_hat = transform(rows_ref, y_ref.at[slot], grad_y)
        x_hat = transform(rows_ref, x_ref.at[slot], conv_in_ref[:, lanes])
        tail_ref[:, lanes] = transform(last_ref, t_ref.at[slot], conv_in_ref[rows - taps:, lanes])
        terms_ref[:, lanes] = correlate(y_hat, x_hat, filter_ref, z_ref.at[slot])

    in_turn(terms_ref.shape[1] // width, width, unit)


def own_input_kernel(place_ref, rows_ref, taps_ref, input_ref, grad_y_ref, *refs):
    pieces, (head_ref, tail_ref, filt_ref, y_ref, f_ref, z_ref, sems) = refs[:-7], refs[-7:]
    channels, width = head_ref.shape[1], y_ref.shape[2]
    copies = []
    for m, piece in enumerate(pieces):
        owner = jnp.bitwise_xor(place_ref[0], m)
        lanes = pl.ds(pl.multiple_of(owner * width, LANE), width)
        copies.append(pltpu.make_async_copy(piece, filt_ref.at[:, lanes], sems.at[m]))
        copies[-1].start()
    for copy in copies:
        copy.wait()

    def unit(which, lanes, slot):
        y_hat = transform(rows_ref, y_ref.at[slot], grad_y_ref[:, lanes])
        f_hat = transform(taps_ref, f_ref.at[slot], filt_ref[:, lanes])
        grad_in = correlate(y_hat, f_hat, input_ref, z_ref.at[slot])
        head_ref[:, lanes] = grad_in[:head_ref.shape[0]].astype(head_ref.dtype)
        tail_ref[:, lanes] = grad_in[head_ref.shape[0]:]

    in_turn(channels // width, width, unit)


def halo_filter_kernel(place_ref, rows_ref, filter_ref, own_ref, x_hat_ref, halo_ref, after_ref,
                       keep_ref, send_ref, y_ref, z_ref, sum_ref):
    del after_ref
    owners, _, width = y_ref.shape
    for which in range(owners):
        lanes = pl.ds(which * width, width)
        y_hat = transform(rows_ref, y_ref.at[which], halo_ref[:, lanes])
        sum_ref[which] = own_ref[:, lanes] + correlate(y_hat, x_hat_ref[:, lanes], filter_ref, z_ref.at[which])
    for pair in range(owners // 2):
        keep_ref[pair] = sum_ref[jnp.bitwise_xor(place_ref[0], 2 * pair)]
        send_ref[pair] = sum_ref[jnp.bitwise_xor(place_ref[0], 2 * pair + 1)].astype(send_ref.dtype)


def halo_input_kernel(rows_ref, taps_ref, input_ref, after_ref, halo_ref, head_ref, tail_ref, filt_ref,
                      order_ref, out_ref, passed_ref, y_ref, f_ref, z_ref, last_ref, sems):
    del order_ref
    head, (owners, _, width) = head_ref.shape[0], y_ref.shape
    taps = halo_ref.shape[0]
    copies = [pltpu.make_async_copy(head_ref, out_ref.at[pl.ds(0, head), :], sems.at[owners])]
    copies[0].start()
    passed_ref[...] = after_ref[...]
    for which in range(owners):
        lanes = pl.ds(which * width, width)
        y_hat = transform(rows_ref, y_ref.at[which], halo_ref[:, lanes])
        f_hat = transform(taps_ref, f_ref.at[which], filt_ref[:, lanes])
        value = tail_ref[:, lanes] + correlate(y_hat, f_hat, input_ref, z_ref.at[which])
        last_ref[:, lanes] = value.astype(last_ref.dtype)
        copies.append(pltpu.make_async_copy(
            last_ref.at[:, lanes], out_ref.at[pl.ds(head, taps), lanes], sems.at[which]
        ))
        copies[-1].start()
    for copy in copies:
        copy.wait()


def scalars():
    return pl.BlockSpec(memory_space=pltpu.SMEM)


def shaped(*shape, dtype=jnp.bfloat16):
    return jax.ShapeDtypeStruct(shape, dtype)


def params():
    return pltpu.CompilerParams(vmem_limit_bytes=14 * 1024 * 1024)


def cost(flops, moved):
    return pl.CostEstimate(flops=flops, bytes_accessed=moved, transcendentals=0)


def make_basis(doc_end, first, rows, taps):
    own = [shaped(2 * rows, 2 * rows), shaped(2 * rows, 2 * taps), shaped(2 * rows, 2 * rows), shaped(2 * taps, 2 * rows)]
    halo = [shaped(2 * taps, 2 * taps)] * 5
    return pl.pallas_call(
        basis_kernel,
        in_specs=[scalars(), scalars()],
        out_shape=own + halo,
        scratch_shapes=[pltpu.VMEM((5, rows, LANE), jnp.int32), pltpu.VMEM((5, 8, rows), jnp.int32)],
        compiler_params=params(),
        cost_estimate=cost(1500000000, 1000000),
        name="basis",
    )(doc_end, first)


def inside(count):
    return [pl.BlockSpec(memory_space=pltpu.VMEM)] * count


def outside(count):
    return [pl.BlockSpec(memory_space=pltpu.HBM)] * count


def held(*shape):
    return pltpu.VMEM(shape, jnp.bfloat16)


def own_filter(bases, grad_out, gate, conv_in, taps, width):
    rows, channels = grad_out.shape
    return pl.pallas_call(
        own_filter_kernel,
        in_specs=inside(6),
        out_specs=inside(3),
        out_shape=[
            shaped(taps, channels, dtype=jnp.float32), shaped(rows, channels),
            shaped(2 * taps, channels, dtype=jnp.float32),
        ],
        scratch_shapes=[
            held(2, 2 * rows, width), held(2, 2 * rows, width), held(2, 2 * taps, width),
            held(2, 2, 2 * rows, width),
        ],
        compiler_params=params(),
        cost_estimate=cost(20 * rows * rows * channels, (6 * rows + 4 * taps) * channels),
        name="own_filter",
    )(*bases, grad_out, gate, conv_in)


def own_input(place, bases, grad_y, pieces):
    rows, channels = grad_y.shape
    taps, width = pieces[0].shape
    return pl.pallas_call(
        own_input_kernel,
        in_specs=[scalars(), *inside(4), *outside(len(pieces))],
        out_specs=inside(3),
        out_shape=[
            shaped(rows - taps, channels), shaped(taps, channels, dtype=jnp.float32), shaped(taps, channels)
        ],
        scratch_shapes=[
            held(2, 2 * rows, width), held(2, 2 * taps, width), held(2, 2, 2 * rows, width),
            pltpu.SemaphoreType.DMA((len(pieces),)),
        ],
        compiler_params=params(),
        cost_estimate=cost(30 * rows * rows * channels, (6 * rows + 6 * taps) * channels),
        name="own_input",
    )(place, *bases, grad_y, *pieces)


def halo_filter(place, bases, own, x_hat, halo, after, owners):
    taps, channels = halo.shape
    width = channels // owners
    return pl.pallas_call(
        halo_filter_kernel,
        in_specs=[scalars(), *inside(6)],
        out_specs=inside(2),
        out_shape=[shaped(owners // 2, taps, width, dtype=jnp.float32), shaped(owners // 2, taps, width)],
        scratch_shapes=[
            held(owners, 2 * taps, width), held(owners, 2, 2 * taps, width),
            pltpu.VMEM((owners, taps, width), jnp.float32),
        ],
        compiler_params=params(),
        cost_estimate=cost(20 * taps * taps * channels, 10 * taps * channels),
        name="halo_filter",
    )(place, *bases, own, x_hat, halo, after)


def halo_input(bases, after, halo, head, tail, filt, order, owners):
    taps, channels = halo.shape
    width = channels // owners
    rows = head.shape[0] + taps
    return pl.pallas_call(
        halo_input_kernel,
        in_specs=[*inside(8), *outside(1)],
        out_specs=[pl.BlockSpec(memory_space=pl.ANY), *inside(1)],
        out_shape=[shaped(rows, channels), shaped(*after.shape, dtype=after.dtype)],
        scratch_shapes=[
            held(owners, 2 * taps, width), held(owners, 2 * taps, width), held(owners, 2, 2 * taps, width),
            held(taps, channels), pltpu.SemaphoreType.DMA((owners + 1,)),
        ],
        compiler_params=params(),
        cost_estimate=cost(28 * taps * taps * channels, 10 * taps * channels),
        name="halo_input",
    )(*bases, after, halo, head, tail, filt, order)


def swap(value, axis, bit):
    return lax.ppermute(value, axis, [(source, source ^ bit) for source in range(lax.axis_size(axis))])


def narrow(value):
    return value.astype(jnp.bfloat16)


def widen(value):
    return value.astype(jnp.float32)


def body(grad_out, gate, conv_in, filt, doc_end):
    rows, channels = grad_out.shape
    taps = filt.shape[1]
    dp, ctx = lax.axis_size("dp"), lax.axis_size("ctx")
    owner, block = lax.axis_index("dp"), lax.axis_index("ctx")
    place = owner.reshape(1)
    first_row = ((owner * ctx + block) * rows).reshape(1)

    following = narrow(widen(grad_out[:taps]) * widen(gate[:taps]))
    halo = lax.ppermute(following, "ctx", [(source, source - 1) for source in range(1, ctx)])
    mine = filt.T
    pieces = [mine] + [swap(mine, "dp", m) for m in range(1, dp)]

    bases = make_basis(doc_end, first_row, rows, taps)
    halo_rows, halo_tail, halo_taps, halo_inverse_input, halo_inverse_filter = bases[4:]
    own, grad_y, x_hat = own_filter((bases[0], bases[3], halo_tail), grad_out, gate, conv_in, taps, channels // dp)
    head, tail, whole_filter = own_input(place, bases[:3], grad_y, pieces)
    keep, send = halo_filter(place, (halo_rows, halo_inverse_filter), own, x_hat, halo, tail, dp)

    bit = 1
    while bit < dp // 2:
        total = keep + widen(swap(send, "dp", bit))
        keep, send = total[0::2], narrow(total[1::2])
        bit *= 2
    half = taps // 2
    low = lax.rem(block, 2) == 0
    home = lambda value: jnp.where(low, value[0, :half], value[0, half:])
    away = lambda value: jnp.where(low, value[0, half:], value[0, :half])
    arrived_away, arrived_home = swap(away(send), "dp", bit), swap(home(send), "dp", bit)
    passing = narrow(away(keep) + widen(arrived_away))
    arrived = swap(passing, "ctx", 1)
    grad_in, kept = halo_input(
        (halo_rows, halo_taps, halo_inverse_input), home(keep), halo, head, tail, whole_filter, passing, dp
    )
    total = kept + widen(arrived_home) + widen(arrived)
    bit = 2
    while bit < ctx:
        mine = narrow(total)
        total = widen(mine) + widen(swap(mine, "ctx", bit))
        bit *= 2
    mine = narrow(total)
    other = swap(mine, "ctx", 1)
    both = jnp.concatenate([jnp.where(low, mine, other), jnp.where(low, other, mine)])
    return (grad_in, widen(both).T)


def solution(mesh):
    placed = (
        P(("dp", "ctx"), None),
        P(("dp", "ctx"), None),
        P(("dp", "ctx"), None),
        P("dp", None),
        P(("dp", "ctx")),
    )
    return jax.shard_map(
        body,
        mesh=mesh,
        in_specs=placed,
        out_specs=(P(("dp", "ctx"), None), P("dp", None)),
        check_vma=False,
    )
```

```python
import math

import jax
import jax.numpy as jnp
from jax import lax
from jax.experimental import pallas as pl
from jax.experimental.pallas import tpu as pltpu
from jax.sharding import PartitionSpec as P

LANE = 128


def half_wave(value):
    square = value * value
    total = jnp.zeros_like(value)
    for power in (13, 11, 9, 7, 5, 3, 1):
        sign = -1.0 if power % 4 == 3 else 1.0
        total = total * square + sign * (2 * math.pi) ** power / math.factorial(power)
    return total * value


def waves(turns):
    size = jnp.abs(turns)
    folded = jnp.minimum(size, 0.5 - size)
    return half_wave(0.25 - size), half_wave(jnp.where(turns < 0.0, -folded, folded))


def two_parts(value):
    high = value.astype(jnp.bfloat16)
    return high, (value - high.astype(jnp.float32)).astype(jnp.bfloat16)


def turns_of(order, offset, size):
    inverse = 1.0 / size.astype(jnp.float32)
    product = (order * offset).astype(jnp.float32)
    whole = jnp.floor(product * inverse + 0.5)
    return (product - whole * size.astype(jnp.float32)) * inverse, inverse


def iota(shape, axis):
    return lax.broadcasted_iota(jnp.int32, shape, axis)


def store_narrow(ref, taps, waves_of):
    bins = ref.shape[0] // 2
    first = iota((bins, 2 * taps), 1) < taps
    for which, wave in enumerate(waves_of):
        high, low = two_parts(wave)
        both = jnp.where(first, high.astype(jnp.float32), low.astype(jnp.float32))
        ref[which * bins:(which + 1) * bins, :] = both.astype(jnp.bfloat16)


def store_back(ref, which, wave):
    count, bins = wave.shape
    ref[0:count, which * bins:(which + 1) * bins], ref[count:2 * count, which * bins:(which + 1) * bins] = two_parts(wave)


def basis_kernel(end_ref, first_ref, rows_ref, taps_ref, input_ref, filter_ref,
                 halo_rows_ref, halo_tail_ref, halo_taps_ref, halo_input_ref, halo_filter_ref, down_ref, across_ref):
    rows, taps = input_ref.shape[0] // 2, filter_ref.shape[0] // 2
    bins = rows
    for ref in (down_ref, across_ref):
        ref[...] = jnp.zeros_like(ref)
        ref[2] = jnp.ones_like(ref[2])

    def document(state):
        start, base, _ = state
        end = jnp.minimum(end_ref[start] - first_ref[0], rows)
        length = end - start
        lags = jnp.minimum(taps, length)
        size = length + lags - 1
        size = size + 1 - lax.rem(size, 2)
        count = (size + 1) // 2
        for ref, axis in ((down_ref, 0), (across_ref, 1)):
            at = iota(ref.shape[1:], axis)
            mine = (at >= base) & (at < base + count)
            for which, value in enumerate((start, end, size, at - base, lags)):
                ref[which] = jnp.where(mine, value, ref[which])
        return end, base + count, start

    start_state = (jnp.int32(0), jnp.int32(0), jnp.int32(0))
    _, _, last_start = lax.while_loop(lambda state: state[0] < rows, document, start_state)

    start, end, size, order, lags = [down_ref[which] for which in range(5)]
    for block in range(rows // LANE):
        at = iota(start.shape, 1) + block * LANE
        inside = (at >= start) & (at < end)
        for which, wave in enumerate(waves(turns_of(order, at - start, size)[0])):
            high, low = two_parts(jnp.where(inside, wave, 0.0))
            below, lanes = which * bins, block * LANE
            rows_ref[below:below + bins, lanes:lanes + LANE] = high
            rows_ref[below:below + bins, rows + lanes:rows + lanes + LANE] = low
    narrow = start[:, 0:2 * taps].shape
    at = iota(narrow, 1)
    at = jnp.where(at < taps, at, at - taps)
    inside = at < lags[:, 0:2 * taps]
    turned = waves(turns_of(order[:, 0:2 * taps], at, size[:, 0:2 * taps])[0])
    store_narrow(taps_ref, taps, [jnp.where(inside, wave, 0.0) for wave in turned])

    start, end, size, order, lags = [across_ref[which, 0:1, :] for which in range(5)]
    for ref, count in ((input_ref, rows), (filter_ref, taps)):
        at = iota((count, bins), 0)
        if ref is input_ref:
            offset, inside = at - start, (at >= start) & (at < end)
        else:
            offset, inside = at, at < lags
        turns, inverse = turns_of(order, offset, size)
        weight = jnp.where(inside, jnp.where(order == 0, inverse, 2.0 * inverse), 0.0)
        for which, wave in enumerate(waves(turns)):
            store_back(ref, which, weight * wave)

    end = jnp.minimum(end_ref[rows - 1] - first_ref[0] - rows, taps - 1)
    begin = jnp.where(end > 0, last_start - (rows - taps), taps)
    size = jnp.full((taps, 2 * taps), 2 * taps - 1, jnp.int32)
    at = iota(size.shape, 1)
    at = jnp.where(at < taps, at, at - taps)
    turned = waves(turns_of(iota(size.shape, 0), at, size)[0])
    store_narrow(halo_taps_ref, taps, turned)
    store_narrow(halo_rows_ref, taps, [jnp.where(at < end, wave, 0.0) for wave in turned])
    store_narrow(halo_tail_ref, taps, [jnp.where(at >= begin, wave, 0.0) for wave in turned])
    size = jnp.full((taps, taps), 2 * taps - 1, jnp.int32)
    at, order = iota(size.shape, 0), iota(size.shape, 1)
    turns, inverse = turns_of(order, at - taps, size)
    weight = jnp.where(at > 0, jnp.where(order == 0, inverse, 2.0 * inverse), 0.0)
    for which, wave in enumerate(waves(turns)):
        store_back(halo_filter_ref, which, weight * wave)
        store_back(halo_input_ref, which, jnp.where(at >= begin, weight * wave, 0.0))


def product(left, right):
    return jnp.dot(left, right, preferred_element_type=jnp.float32)


def transform(basis_ref, twice_ref, value):
    twice(twice_ref, value)
    return product(basis_ref[...], twice_ref[...])


def correlate(left, right, basis_ref, z_ref):
    bins, count = left.shape[0] // 2, basis_ref.shape[0] // 2
    lc, ls, rc, rs = left[:bins], left[bins:], right[:bins], right[bins:]
    z_ref[0, 0:bins, :], z_ref[1, 0:bins, :] = two_parts(lc * rc + ls * rs)
    z_ref[0, bins:, :], z_ref[1, bins:, :] = two_parts(ls * rc - lc * rs)
    both = product(basis_ref[...], z_ref[0])
    return both[:count] + (both[count:] + product(basis_ref[0:count, :], z_ref[1]))


def twice(ref, value):
    count = value.shape[0]
    ref[0:count, :] = value
    ref[count:2 * count, :] = value


def gated(grad_out, gate):
    return (grad_out.astype(jnp.float32) * gate.astype(jnp.float32)).astype(jnp.bfloat16)


def in_turn(count, width, unit):
    together = 2 if count % 2 == 0 else 1

    def step(at, carry):
        for slot in range(together):
            which = at * together + slot
            unit(which, pl.ds(pl.multiple_of(which * width, LANE), width), slot)
        return carry

    lax.fori_loop(0, count // together, step, 0)


def own_filter_kernel(rows_ref, filter_ref, last_ref, grad_out_ref, gate_ref, conv_in_ref, terms_ref, grad_y_ref, tail_ref,
                      y_ref, x_ref, t_ref, z_ref):
    width, taps, rows = y_ref.shape[2], terms_ref.shape[0], grad_y_ref.shape[0]

    def unit(which, lanes, slot):
        grad_y = gated(grad_out_ref[:, lanes], gate_ref[:, lanes])
        grad_y_ref[:, lanes] = grad_y
        y_hat = transform(rows_ref, y_ref.at[slot], grad_y)
        x_hat = transform(rows_ref, x_ref.at[slot], conv_in_ref[:, lanes])
        tail_ref[:, lanes] = transform(last_ref, t_ref.at[slot], conv_in_ref[rows - taps:, lanes])
        terms_ref[:, lanes] = correlate(y_hat, x_hat, filter_ref, z_ref.at[slot])

    in_turn(terms_ref.shape[1] // width, width, unit)


def own_input_kernel(place_ref, rows_ref, taps_ref, input_ref, grad_y_ref, *refs):
    pieces, (head_ref, tail_ref, filt_ref, y_ref, f_ref, z_ref, sems) = refs[:-7], refs[-7:]
    channels, width = head_ref.shape[1], y_ref.shape[2]
    copies = []
    for m, piece in enumerate(pieces):
        owner = jnp.bitwise_xor(place_ref[0], m)
        lanes = pl.ds(pl.multiple_of(owner * width, LANE), width)
        copies.append(pltpu.make_async_copy(piece, filt_ref.at[:, lanes], sems.at[m]))
        copies[-1].start()
    for copy in copies:
        copy.wait()

    def unit(which, lanes, slot):
        y_hat = transform(rows_ref, y_ref.at[slot], grad_y_ref[:, lanes])
        f_hat = transform(taps_ref, f_ref.at[slot], filt_ref[:, lanes])
        grad_in = correlate(y_hat, f_hat, input_ref, z_ref.at[slot])
        head_ref[:, lanes] = grad_in[:head_ref.shape[0]].astype(head_ref.dtype)
        tail_ref[:, lanes] = grad_in[head_ref.shape[0]:]

    in_turn(channels // width, width, unit)


def halo_filter_kernel(place_ref, rows_ref, filter_ref, own_ref, x_hat_ref, halo_ref, after_ref,
                       keep_ref, send_ref, y_ref, z_ref, sum_ref):
    del after_ref
    owners, _, width = y_ref.shape
    for which in range(owners):
        lanes = pl.ds(which * width, width)
        y_hat = transform(rows_ref, y_ref.at[which], halo_ref[:, lanes])
        sum_ref[which] = own_ref[:, lanes] + correlate(y_hat, x_hat_ref[:, lanes], filter_ref, z_ref.at[which])
    for pair in range(owners // 2):
        keep_ref[pair] = sum_ref[jnp.bitwise_xor(place_ref[0], 2 * pair)]
        send_ref[pair] = sum_ref[jnp.bitwise_xor(place_ref[0], 2 * pair + 1)].astype(send_ref.dtype)


def split_kernel(home_ref, keep_ref, arrived_ref, away_ref, stay_ref, kept_away_ref, kept_stay_ref):
    part = away_ref.shape[0]
    home = pl.multiple_of(home_ref[0], part)
    for offset, send_ref, kept_ref in ((part - home, away_ref, kept_away_ref), (home, stay_ref, kept_stay_ref)):
        rows = pl.ds(pl.multiple_of(offset, part), part)
        kept_ref[...] = keep_ref[0, rows, :] + arrived_ref[0, rows, :].astype(jnp.float32)
        send_ref[...] = (keep_ref[1, rows, :] + arrived_ref[1, rows, :].astype(jnp.float32)).astype(send_ref.dtype)


def halo_input_kernel(rows_ref, taps_ref, input_ref, after_ref, halo_ref, head_ref, tail_ref, filt_ref,
                      order_ref, out_ref, passed_ref, y_ref, f_ref, z_ref, last_ref, sems):
    del order_ref
    head, (owners, _, width) = head_ref.shape[0], y_ref.shape
    taps = halo_ref.shape[0]
    copies = [pltpu.make_async_copy(head_ref, out_ref.at[pl.ds(0, head), :], sems.at[owners])]
    copies[0].start()
    passed_ref[...] = after_ref[...]
    for which in range(owners):
        lanes = pl.ds(which * width, width)
        y_hat = transform(rows_ref, y_ref.at[which], halo_ref[:, lanes])
        f_hat = transform(taps_ref, f_ref.at[which], filt_ref[:, lanes])
        value = tail_ref[:, lanes] + correlate(y_hat, f_hat, input_ref, z_ref.at[which])
        last_ref[:, lanes] = value.astype(last_ref.dtype)
        copies.append(pltpu.make_async_copy(
            last_ref.at[:, lanes], out_ref.at[pl.ds(head, taps), lanes], sems.at[which]
        ))
        copies[-1].start()
    for copy in copies:
        copy.wait()


def scalars():
    return pl.BlockSpec(memory_space=pltpu.SMEM)


def shaped(*shape, dtype=jnp.bfloat16):
    return jax.ShapeDtypeStruct(shape, dtype)


def params():
    return pltpu.CompilerParams(vmem_limit_bytes=14 * 1024 * 1024)


def cost(flops, moved):
    return pl.CostEstimate(flops=flops, bytes_accessed=moved, transcendentals=0)


def make_basis(doc_end, first, rows, taps):
    own = [shaped(2 * rows, 2 * rows), shaped(2 * rows, 2 * taps), shaped(2 * rows, 2 * rows), shaped(2 * taps, 2 * rows)]
    halo = [shaped(2 * taps, 2 * taps)] * 5
    return pl.pallas_call(
        basis_kernel,
        in_specs=[scalars(), scalars()],
        out_shape=own + halo,
        scratch_shapes=[pltpu.VMEM((5, rows, LANE), jnp.int32), pltpu.VMEM((5, 8, rows), jnp.int32)],
        compiler_params=params(),
        cost_estimate=cost(1500000000, 1000000),
        name="basis",
    )(doc_end, first)


def inside(count):
    return [pl.BlockSpec(memory_space=pltpu.VMEM)] * count


def outside(count):
    return [pl.BlockSpec(memory_space=pltpu.HBM)] * count


def held(*shape):
    return pltpu.VMEM(shape, jnp.bfloat16)


def own_filter(bases, grad_out, gate, conv_in, taps, width):
    rows, channels = grad_out.shape
    return pl.pallas_call(
        own_filter_kernel,
        in_specs=inside(6),
        out_specs=inside(3),
        out_shape=[
            shaped(taps, channels, dtype=jnp.float32), shaped(rows, channels),
            shaped(2 * taps, channels, dtype=jnp.float32),
        ],
        scratch_shapes=[
            held(2, 2 * rows, width), held(2, 2 * rows, width), held(2, 2 * taps, width),
            held(2, 2, 2 * rows, width),
        ],
        compiler_params=params(),
        cost_estimate=cost(20 * rows * rows * channels, (6 * rows + 4 * taps) * channels),
        name="own_filter",
    )(*bases, grad_out, gate, conv_in)


def own_input(place, bases, grad_y, pieces):
    rows, channels = grad_y.shape
    taps, width = pieces[0].shape
    return pl.pallas_call(
        own_input_kernel,
        in_specs=[scalars(), *inside(4), *outside(len(pieces))],
        out_specs=inside(3),
        out_shape=[
            shaped(rows - taps, channels), shaped(taps, channels, dtype=jnp.float32), shaped(taps, channels)
        ],
        scratch_shapes=[
            held(2, 2 * rows, width), held(2, 2 * taps, width), held(2, 2, 2 * rows, width),
            pltpu.SemaphoreType.DMA((len(pieces),)),
        ],
        compiler_params=params(),
        cost_estimate=cost(30 * rows * rows * channels, (6 * rows + 6 * taps) * channels),
        name="own_input",
    )(place, *bases, grad_y, *pieces)


def halo_filter(place, bases, own, x_hat, halo, after, owners):
    taps, channels = halo.shape
    width = channels // owners
    return pl.pallas_call(
        halo_filter_kernel,
        in_specs=[scalars(), *inside(6)],
        out_specs=inside(2),
        out_shape=[shaped(owners // 2, taps, width, dtype=jnp.float32), shaped(owners // 2, taps, width)],
        scratch_shapes=[
            held(owners, 2 * taps, width), held(owners, 2, 2 * taps, width),
            pltpu.VMEM((owners, taps, width), jnp.float32),
        ],
        compiler_params=params(),
        cost_estimate=cost(20 * taps * taps * channels, 10 * taps * channels),
        name="halo_filter",
    )(place, *bases, own, x_hat, halo, after)


def split(home, keep, arrived):
    _, taps, width = keep.shape
    halves = [shaped(taps // 2, width)] * 2 + [shaped(taps // 2, width, dtype=jnp.float32)] * 2
    return pl.pallas_call(
        split_kernel,
        in_specs=[scalars(), *inside(2)],
        out_specs=inside(4),
        out_shape=halves,
        compiler_params=params(),
        cost_estimate=cost(4 * taps * width, 16 * taps * width),
        name="split",
    )(home, keep, arrived)


def halo_input(bases, after, halo, head, tail, filt, order, owners):
    taps, channels = halo.shape
    width = channels // owners
    rows = head.shape[0] + taps
    return pl.pallas_call(
        halo_input_kernel,
        in_specs=[*inside(8), *outside(1)],
        out_specs=[pl.BlockSpec(memory_space=pl.ANY), *inside(1)],
        out_shape=[shaped(rows, channels), shaped(*after.shape, dtype=after.dtype)],
        scratch_shapes=[
            held(owners, 2 * taps, width), held(owners, 2 * taps, width), held(owners, 2, 2 * taps, width),
            held(taps, channels), pltpu.SemaphoreType.DMA((owners + 1,)),
        ],
        compiler_params=params(),
        cost_estimate=cost(28 * taps * taps * channels, 10 * taps * channels),
        name="halo_input",
    )(*bases, after, halo, head, tail, filt, order)


def swap(value, axis, bit):
    return lax.ppermute(value, axis, [(source, source ^ bit) for source in range(lax.axis_size(axis))])


def narrow(value):
    return value.astype(jnp.bfloat16)


def widen(value):
    return value.astype(jnp.float32)


def body(grad_out, gate, conv_in, filt, doc_end):
    rows, channels = grad_out.shape
    taps = filt.shape[1]
    dp, ctx = lax.axis_size("dp"), lax.axis_size("ctx")
    owner, block = lax.axis_index("dp"), lax.axis_index("ctx")
    place = owner.reshape(1)
    first_row = ((owner * ctx + block) * rows).reshape(1)

    following = narrow(widen(grad_out[:taps]) * widen(gate[:taps]))
    halo = lax.ppermute(following, "ctx", [(source, source - 1) for source in range(1, ctx)])
    mine = filt.T
    pieces = [mine] + [swap(mine, "dp", m) for m in range(1, dp)]

    bases = make_basis(doc_end, first_row, rows, taps)
    halo_rows, halo_tail, halo_taps, halo_inverse_input, halo_inverse_filter = bases[4:]
    own, grad_y, x_hat = own_filter((bases[0], bases[3], halo_tail), grad_out, gate, conv_in, taps, channels // dp)
    head, tail, whole_filter = own_input(place, bases[:3], grad_y, pieces)
    keep, send = halo_filter(place, (halo_rows, halo_inverse_filter), own, x_hat, halo, tail, dp)

    bit = 1
    while bit < dp // 4:
        total = keep + widen(swap(send, "dp", bit))
        keep, send = total[0::2], narrow(total[1::2])
        bit *= 2
    low = lax.rem(block, 2) == 0
    home = jnp.where(low, 0, taps // 2).reshape(1)
    away, stay, kept_away, kept = split(home, keep, swap(send, "dp", bit))
    arrived_away, arrived_home = swap(away, "dp", 2 * bit), swap(stay, "dp", 2 * bit)
    passing = narrow(kept_away + widen(arrived_away))
    arrived = swap(passing, "ctx", 1)
    grad_in, kept = halo_input(
        (halo_rows, halo_taps, halo_inverse_input), kept, halo, head, tail, whole_filter, passing, dp
    )
    total = kept + widen(arrived_home) + widen(arrived)
    bit = 2
    while bit < ctx:
        mine = narrow(total)
        total = widen(mine) + widen(swap(mine, "ctx", bit))
        bit *= 2
    mine = narrow(total)
    other = swap(mine, "ctx", 1)
    both = jnp.concatenate([jnp.where(low, mine, other), jnp.where(low, other, mine)])
    return (grad_in, widen(both).T)


def solution(mesh):
    placed = (
        P(("dp", "ctx"), None),
        P(("dp", "ctx"), None),
        P(("dp", "ctx"), None),
        P("dp", None),
        P(("dp", "ctx")),
    )
    return jax.shard_map(
        body,
        mesh=mesh,
        in_specs=placed,
        out_specs=(P(("dp", "ctx"), None), P("dp", None)),
        check_vma=False,
    )
```

```python
import math

import jax
import jax.numpy as jnp
from jax import lax
from jax.experimental import pallas as pl
from jax.experimental.pallas import tpu as pltpu
from jax.sharding import PartitionSpec as P

LANE = 128


def half_wave(value):
    square = value * value
    total = jnp.zeros_like(value)
    for power in (13, 11, 9, 7, 5, 3, 1):
        sign = -1.0 if power % 4 == 3 else 1.0
        total = total * square + sign * (2 * math.pi) ** power / math.factorial(power)
    return total * value


def waves(turns):
    size = jnp.abs(turns)
    folded = jnp.minimum(size, 0.5 - size)
    return half_wave(0.25 - size), half_wave(jnp.where(turns < 0.0, -folded, folded))


def two_parts(value):
    high = value.astype(jnp.bfloat16)
    return high, (value - high.astype(jnp.float32)).astype(jnp.bfloat16)


def turns_of(order, offset, size):
    inverse = 1.0 / size.astype(jnp.float32)
    product = (order * offset).astype(jnp.float32)
    whole = jnp.floor(product * inverse + 0.5)
    return (product - whole * size.astype(jnp.float32)) * inverse, inverse


def iota(shape, axis):
    return lax.broadcasted_iota(jnp.int32, shape, axis)


def store_narrow(ref, taps, waves_of):
    bins = ref.shape[0] // 2
    first = iota((bins, 2 * taps), 1) < taps
    for which, wave in enumerate(waves_of):
        high, low = two_parts(wave)
        both = jnp.where(first, high.astype(jnp.float32), low.astype(jnp.float32))
        ref[which * bins:(which + 1) * bins, :] = both.astype(jnp.bfloat16)


def store_back(ref, which, wave):
    count, bins = wave.shape
    ref[0:count, which * bins:(which + 1) * bins], ref[count:2 * count, which * bins:(which + 1) * bins] = two_parts(wave)


def basis_kernel(end_ref, first_ref, rows_ref, taps_ref, input_ref, filter_ref,
                 halo_rows_ref, halo_tail_ref, halo_taps_ref, halo_input_ref, halo_filter_ref, down_ref, across_ref):
    rows, taps = input_ref.shape[0] // 2, filter_ref.shape[0] // 2
    bins = rows
    for ref in (down_ref, across_ref):
        ref[...] = jnp.zeros_like(ref)
        ref[2] = jnp.ones_like(ref[2])

    def document(state):
        start, base, _ = state
        end = jnp.minimum(end_ref[start] - first_ref[0], rows)
        length = end - start
        lags = jnp.minimum(taps, length)
        size = length + lags - 1
        size = size + 1 - lax.rem(size, 2)
        count = (size + 1) // 2
        for ref, axis in ((down_ref, 0), (across_ref, 1)):
            at = iota(ref.shape[1:], axis)
            mine = (at >= base) & (at < base + count)
            for which, value in enumerate((start, end, size, at - base, lags)):
                ref[which] = jnp.where(mine, value, ref[which])
        return end, base + count, start

    start_state = (jnp.int32(0), jnp.int32(0), jnp.int32(0))
    _, _, last_start = lax.while_loop(lambda state: state[0] < rows, document, start_state)

    start, end, size, order, lags = [down_ref[which] for which in range(5)]
    for block in range(rows // LANE):
        at = iota(start.shape, 1) + block * LANE
        inside = (at >= start) & (at < end)
        for which, wave in enumerate(waves(turns_of(order, at - start, size)[0])):
            high, low = two_parts(jnp.where(inside, wave, 0.0))
            below, lanes = which * bins, block * LANE
            rows_ref[below:below + bins, lanes:lanes + LANE] = high
            rows_ref[below:below + bins, rows + lanes:rows + lanes + LANE] = low
    narrow = start[:, 0:2 * taps].shape
    at = iota(narrow, 1)
    at = jnp.where(at < taps, at, at - taps)
    inside = at < lags[:, 0:2 * taps]
    turned = waves(turns_of(order[:, 0:2 * taps], at, size[:, 0:2 * taps])[0])
    store_narrow(taps_ref, taps, [jnp.where(inside, wave, 0.0) for wave in turned])

    start, end, size, order, lags = [across_ref[which, 0:1, :] for which in range(5)]
    for ref, count in ((input_ref, rows), (filter_ref, taps)):
        at = iota((count, bins), 0)
        if ref is input_ref:
            offset, inside = at - start, (at >= start) & (at < end)
        else:
            offset, inside = at, at < lags
        turns, inverse = turns_of(order, offset, size)
        weight = jnp.where(inside, jnp.where(order == 0, inverse, 2.0 * inverse), 0.0)
        for which, wave in enumerate(waves(turns)):
            store_back(ref, which, weight * wave)

    end = jnp.minimum(end_ref[rows - 1] - first_ref[0] - rows, taps - 1)
    begin = jnp.where(end > 0, last_start - (rows - taps), taps)
    size = jnp.full((taps, 2 * taps), 2 * taps - 1, jnp.int32)
    at = iota(size.shape, 1)
    at = jnp.where(at < taps, at, at - taps)
    turned = waves(turns_of(iota(size.shape, 0), at, size)[0])
    store_narrow(halo_taps_ref, taps, turned)
    store_narrow(halo_rows_ref, taps, [jnp.where(at < end, wave, 0.0) for wave in turned])
    store_narrow(halo_tail_ref, taps, [jnp.where(at >= begin, wave, 0.0) for wave in turned])
    size = jnp.full((taps, taps), 2 * taps - 1, jnp.int32)
    at, order = iota(size.shape, 0), iota(size.shape, 1)
    turns, inverse = turns_of(order, at - taps, size)
    weight = jnp.where(at > 0, jnp.where(order == 0, inverse, 2.0 * inverse), 0.0)
    for which, wave in enumerate(waves(turns)):
        store_back(halo_filter_ref, which, weight * wave)
        store_back(halo_input_ref, which, jnp.where(at >= begin, weight * wave, 0.0))


def product(left, right):
    return jnp.dot(left, right, preferred_element_type=jnp.float32)


def transform(basis_ref, twice_ref, value):
    twice(twice_ref, value)
    return product(basis_ref[...], twice_ref[...])


def correlate(left, right, basis_ref, z_ref):
    bins, count = left.shape[0] // 2, basis_ref.shape[0] // 2
    lc, ls, rc, rs = left[:bins], left[bins:], right[:bins], right[bins:]
    z_ref[0, 0:bins, :], z_ref[1, 0:bins, :] = two_parts(lc * rc + ls * rs)
    z_ref[0, bins:, :], z_ref[1, bins:, :] = two_parts(ls * rc - lc * rs)
    both = product(basis_ref[...], z_ref[0])
    return both[:count] + (both[count:] + product(basis_ref[0:count, :], z_ref[1]))


def twice(ref, value):
    count = value.shape[0]
    ref[0:count, :] = value
    ref[count:2 * count, :] = value


def gated(grad_out, gate):
    return (grad_out.astype(jnp.float32) * gate.astype(jnp.float32)).astype(jnp.bfloat16)


def in_turn(count, width, unit):
    together = 2 if count % 2 == 0 else 1

    def step(at, carry):
        for slot in range(together):
            which = at * together + slot
            unit(which, pl.ds(pl.multiple_of(which * width, LANE), width), slot)
        return carry

    lax.fori_loop(0, count // together, step, 0)


def own_filter_kernel(rows_ref, filter_ref, last_ref, grad_out_ref, gate_ref, conv_in_ref, terms_ref, grad_y_ref, tail_ref,
                      y_ref, x_ref, t_ref, z_ref):
    width, taps, rows = y_ref.shape[2], terms_ref.shape[0], grad_y_ref.shape[0]

    def unit(which, lanes, slot):
        grad_y = gated(grad_out_ref[:, lanes], gate_ref[:, lanes])
        grad_y_ref[:, lanes] = grad_y
        y_hat = transform(rows_ref, y_ref.at[slot], grad_y)
        x_hat = transform(rows_ref, x_ref.at[slot], conv_in_ref[:, lanes])
        tail_ref[:, lanes] = transform(last_ref, t_ref.at[slot], conv_in_ref[rows - taps:, lanes])
        terms_ref[:, lanes] = correlate(y_hat, x_hat, filter_ref, z_ref.at[slot])

    in_turn(terms_ref.shape[1] // width, width, unit)


def own_input_kernel(place_ref, rows_ref, taps_ref, input_ref, grad_y_ref, *refs):
    pieces, (head_ref, tail_ref, filt_ref, y_ref, f_ref, z_ref, sems) = refs[:-7], refs[-7:]
    channels, width = head_ref.shape[1], y_ref.shape[2]
    copies = []
    for m, piece in enumerate(pieces):
        owner = jnp.bitwise_xor(place_ref[0], m)
        lanes = pl.ds(pl.multiple_of(owner * width, LANE), width)
        copies.append(pltpu.make_async_copy(piece, filt_ref.at[:, lanes], sems.at[m]))
        copies[-1].start()
    for copy in copies:
        copy.wait()

    def unit(which, lanes, slot):
        y_hat = transform(rows_ref, y_ref.at[slot], grad_y_ref[:, lanes])
        f_hat = transform(taps_ref, f_ref.at[slot], filt_ref[:, lanes])
        grad_in = correlate(y_hat, f_hat, input_ref, z_ref.at[slot])
        head_ref[:, lanes] = grad_in[:head_ref.shape[0]].astype(head_ref.dtype)
        tail_ref[:, lanes] = grad_in[head_ref.shape[0]:]

    in_turn(channels // width, width, unit)


def halo_filter_kernel(place_ref, rows_ref, filter_ref, own_ref, x_hat_ref, halo_ref, after_ref,
                       keep_ref, send_ref, y_ref, z_ref, sum_ref):
    del after_ref
    owners, _, width = y_ref.shape
    for which in range(owners):
        lanes = pl.ds(which * width, width)
        y_hat = transform(rows_ref, y_ref.at[which], halo_ref[:, lanes])
        sum_ref[which] = own_ref[:, lanes] + correlate(y_hat, x_hat_ref[:, lanes], filter_ref, z_ref.at[which])
    for pair in range(owners // 2):
        keep_ref[pair] = sum_ref[jnp.bitwise_xor(place_ref[0], 2 * pair)]
        send_ref[pair] = sum_ref[jnp.bitwise_xor(place_ref[0], 2 * pair + 1)].astype(send_ref.dtype)


def halo_input_kernel(rows_ref, taps_ref, input_ref, after_ref, halo_ref, head_ref, tail_ref, filt_ref,
                      out_ref, passed_ref, y_ref, f_ref, z_ref, last_ref, sems):
    head, (owners, _, width) = head_ref.shape[0], y_ref.shape
    taps = halo_ref.shape[0]
    copies = [pltpu.make_async_copy(head_ref, out_ref.at[pl.ds(0, head), :], sems.at[owners])]
    copies[0].start()
    passed_ref[...] = after_ref[...]
    for which in range(owners):
        lanes = pl.ds(which * width, width)
        y_hat = transform(rows_ref, y_ref.at[which], halo_ref[:, lanes])
        f_hat = transform(taps_ref, f_ref.at[which], filt_ref[:, lanes])
        value = tail_ref[:, lanes] + correlate(y_hat, f_hat, input_ref, z_ref.at[which])
        last_ref[:, lanes] = value.astype(last_ref.dtype)
        copies.append(pltpu.make_async_copy(
            last_ref.at[:, lanes], out_ref.at[pl.ds(head, taps), lanes], sems.at[which]
        ))
        copies[-1].start()
    for copy in copies:
        copy.wait()


def scalars():
    return pl.BlockSpec(memory_space=pltpu.SMEM)


def shaped(*shape, dtype=jnp.bfloat16):
    return jax.ShapeDtypeStruct(shape, dtype)


def params():
    return pltpu.CompilerParams(vmem_limit_bytes=18 * 1024 * 1024)


def cost(flops, moved):
    return pl.CostEstimate(flops=flops, bytes_accessed=moved, transcendentals=0)


def make_basis(doc_end, first, rows, taps):
    own = [shaped(2 * rows, 2 * rows), shaped(2 * rows, 2 * taps), shaped(2 * rows, 2 * rows), shaped(2 * taps, 2 * rows)]
    halo = [shaped(2 * taps, 2 * taps)] * 5
    return pl.pallas_call(
        basis_kernel,
        in_specs=[scalars(), scalars()],
        out_shape=own + halo,
        scratch_shapes=[pltpu.VMEM((5, rows, LANE), jnp.int32), pltpu.VMEM((5, 8, rows), jnp.int32)],
        compiler_params=params(),
        cost_estimate=cost(1500000000, 1000000),
        name="basis",
    )(doc_end, first)


def inside(count):
    return [pl.BlockSpec(memory_space=pltpu.VMEM)] * count


def outside(count):
    return [pl.BlockSpec(memory_space=pltpu.HBM)] * count


def held(*shape):
    return pltpu.VMEM(shape, jnp.bfloat16)


def own_filter(bases, grad_out, gate, conv_in, taps, width):
    rows, channels = grad_out.shape
    return pl.pallas_call(
        own_filter_kernel,
        in_specs=inside(6),
        out_specs=inside(3),
        out_shape=[
            shaped(taps, channels, dtype=jnp.float32), shaped(rows, channels),
            shaped(2 * taps, channels, dtype=jnp.float32),
        ],
        scratch_shapes=[
            held(2, 2 * rows, width), held(2, 2 * rows, width), held(2, 2 * taps, width),
            held(2, 2, 2 * rows, width),
        ],
        compiler_params=params(),
        cost_estimate=cost(20 * rows * rows * channels, (6 * rows + 4 * taps) * channels),
        name="own_filter",
    )(*bases, grad_out, gate, conv_in)


def own_input(place, bases, grad_y, pieces):
    rows, channels = grad_y.shape
    taps, width = pieces[0].shape
    return pl.pallas_call(
        own_input_kernel,
        in_specs=[scalars(), *inside(4), *outside(len(pieces))],
        out_specs=inside(3),
        out_shape=[
            shaped(rows - taps, channels), shaped(taps, channels, dtype=jnp.float32), shaped(taps, channels)
        ],
        scratch_shapes=[
            held(2, 2 * rows, width), held(2, 2 * taps, width), held(2, 2, 2 * rows, width),
            pltpu.SemaphoreType.DMA((len(pieces),)),
        ],
        compiler_params=params(),
        cost_estimate=cost(30 * rows * rows * channels, (6 * rows + 6 * taps) * channels),
        name="own_input",
    )(place, *bases, grad_y, *pieces)


def halo_filter(place, bases, own, x_hat, halo, after, owners):
    taps, channels = halo.shape
    width = channels // owners
    return pl.pallas_call(
        halo_filter_kernel,
        in_specs=[scalars(), *inside(6)],
        out_specs=inside(2),
        out_shape=[shaped(owners // 2, taps, width, dtype=jnp.float32), shaped(owners // 2, taps, width)],
        scratch_shapes=[
            held(owners, 2 * taps, width), held(owners, 2, 2 * taps, width),
            pltpu.VMEM((owners, taps, width), jnp.float32),
        ],
        compiler_params=params(),
        cost_estimate=cost(20 * taps * taps * channels, 10 * taps * channels),
        name="halo_filter",
    )(place, *bases, own, x_hat, halo, after)


def halo_input(bases, after, halo, head, tail, filt, owners):
    taps, channels = halo.shape
    width = channels // owners
    rows = head.shape[0] + taps
    return pl.pallas_call(
        halo_input_kernel,
        in_specs=inside(8),
        out_specs=[pl.BlockSpec(memory_space=pl.ANY), *inside(1)],
        out_shape=[shaped(rows, channels), shaped(*after.shape, dtype=after.dtype)],
        scratch_shapes=[
            held(owners, 2 * taps, width), held(owners, 2 * taps, width), held(owners, 2, 2 * taps, width),
            held(taps, channels), pltpu.SemaphoreType.DMA((owners + 1,)),
        ],
        compiler_params=params(),
        cost_estimate=cost(28 * taps * taps * channels, 10 * taps * channels),
        name="halo_input",
    )(*bases, after, halo, head, tail, filt)


def swap(value, axis, bit):
    return lax.ppermute(value, axis, [(source, source ^ bit) for source in range(lax.axis_size(axis))])


def narrow(value):
    return value.astype(jnp.bfloat16)


def widen(value):
    return value.astype(jnp.float32)


def body(grad_out, gate, conv_in, filt, doc_end):
    rows, channels = grad_out.shape
    taps = filt.shape[1]
    dp, ctx = lax.axis_size("dp"), lax.axis_size("ctx")
    owner, block = lax.axis_index("dp"), lax.axis_index("ctx")
    place = owner.reshape(1)
    first_row = ((owner * ctx + block) * rows).reshape(1)

    following = narrow(widen(grad_out[:taps]) * widen(gate[:taps]))
    halo = lax.ppermute(following, "ctx", [(source, source - 1) for source in range(1, ctx)])
    mine = filt.T
    pieces = [mine] + [swap(mine, "dp", m) for m in range(1, dp)]

    bases = make_basis(doc_end, first_row, rows, taps)
    halo_rows, halo_tail, halo_taps, halo_inverse_input, halo_inverse_filter = bases[4:]
    own, grad_y, x_hat = own_filter((bases[0], bases[3], halo_tail), grad_out, gate, conv_in, taps, channels // dp)
    head, tail, whole_filter = own_input(place, bases[:3], grad_y, pieces)
    keep, send = halo_filter(place, (halo_rows, halo_inverse_filter), own, x_hat, halo, tail, dp)

    arrived, bit = swap(send, "dp", 1), 2
    while bit < dp:
        total = keep + widen(arrived)
        keep, arrived = total[0::2], swap(narrow(total[1::2]), "dp", bit)
        bit *= 2
    grad_in, keep = halo_input(
        (halo_rows, halo_taps, halo_inverse_input), keep, halo, head, tail, whole_filter, dp
    )
    total = (keep + widen(arrived))[0]
    half = taps // 2
    low = lax.rem(block, 2) == 0
    kept = jnp.where(low, total[:half], total[half:])
    total = kept + widen(swap(narrow(jnp.where(low, total[half:], total[:half])), "ctx", 1))
    bit = 2
    while bit < ctx:
        mine = narrow(total)
        total = widen(mine) + widen(swap(mine, "ctx", bit))
        bit *= 2
    mine = narrow(total)
    other = swap(mine, "ctx", 1)
    both = jnp.concatenate([jnp.where(low, mine, other), jnp.where(low, other, mine)])
    return (grad_in, widen(both).T)


def solution(mesh):
    placed = (
        P(("dp", "ctx"), None),
        P(("dp", "ctx"), None),
        P(("dp", "ctx"), None),
        P("dp", None),
        P(("dp", "ctx")),
    )
    return jax.shard_map(
        body,
        mesh=mesh,
        in_specs=placed,
        out_specs=(P(("dp", "ctx"), None), P("dp", None)),
        check_vma=False,
    )
```
